256 devices in a mesh: seq: 64 (over x, z, core), grp: 4 (over y).
Axes of the slice: x: 4, y: 4, z: 8, core: 2. Of those that a mesh axis runs over, the one named last changes fastest.
Arguments:
- queries: bfloat16 [4, 8192, 640], P('grp', 'seq'), may hold values from -120 to 120
- comp_kv: bfloat16 [4, 8192, 256], P('grp', 'seq'), may hold values from -6 to 6
- out_grad: bfloat16 [4, 8192, 640], P('grp', 'seq'), may hold values from -6 to 6
- comp_ids: int32 [4, 8192], P('grp', 'seq'), may hold values from 0 to 7, as said below
- comp_pos: int32 [4, 8192], P('grp', 'seq'), may hold values from 0 to 4095, as said below
- prompt_kv: bfloat16 [4, 4096, 256], P('grp', 'seq'), may hold values from -6 to 6
- owned_prompt: int32 [4], replicated, may hold values from 0 to 3, each once
Outputs:
- grad_queries: bfloat16 [4, 8192, 640], P('grp', 'seq')
- grad_comp_kv: bfloat16 [4, 8192, 256], P('grp', 'seq')
- grad_prompt_kv: bfloat16 [4, 4096, 256], P('grp', 'seq')
The draws below stay inside these ranges and needn't reach their ends.
Inputs may be any that keep to these rules, and one draw needn't show every extreme that they name: `comp_ids`: completions 0 to 7 each hold whole blocks of 32 consecutive positions; each is packed in blocks of 32 tokens in an arbitrary order over the token axis; the longest completion has exactly 128 blocks. `comp_pos`: the tokens of one completion hold positions 0 to its length minus one, each once.
All inputs are finite; a program needn't handle non-finite values.
Results may differ from the reference program's by a relative error of at most 0.005.
Values may be sent and summed in bfloat16 or wider, within the bound.
A program may use at most 128 MiB of HBM per device.

```python
import math
import jax
import jax.numpy as jnp
from jax import lax

H = 5
DH = 128
COMPS = 8
BLK = 32
TOK_DEV = 128
PROMPTS = 4
PLEN = 4096
CTOK = 8192


def packing(key):
    key = jax.random.fold_in(key, 101)
    nblocks = CTOK // BLK
    longest = nblocks // 2

    def single(prompt_key):
        cut_key, order_key = jax.random.split(prompt_key)
        rest = jax.random.permutation(cut_key, nblocks - longest - 1)[:COMPS - 2] + longest + 1
        cuts = jnp.sort(jnp.concatenate([jnp.full((1,), longest, jnp.int32), rest.astype(jnp.int32)])).astype(jnp.int32)
        blocks = jnp.arange(nblocks, dtype=jnp.int32)
        comp_of_block = jnp.sum((blocks[:, None] >= cuts[None, :]).astype(jnp.int32), 1)
        starts = jnp.concatenate([jnp.zeros((1,), jnp.int32), cuts])
        start_of_block = starts[comp_of_block]
        order = jax.random.permutation(order_key, nblocks).astype(jnp.int32)
        block_comp = comp_of_block[order]
        block_first = (order - start_of_block[order]) * BLK
        ids = jnp.repeat(block_comp, BLK)
        within = jnp.tile(jnp.arange(BLK, dtype=jnp.int32), nblocks)
        positions = jnp.repeat(block_first, BLK) + within
        return (ids, positions)
    return jax.vmap(single)(jax.random.split(key, PROMPTS))


def key_base(key):
    key = jax.random.fold_in(key, 202)
    return jnp.clip(jax.random.normal(key, (PROMPTS, CTOK, DH), jnp.float32), -6.0, 6.0)


def draw_comp_ids(key, part):
    return packing(key)[0].astype(jnp.int32)


def draw_comp_pos(key, part):
    return packing(key)[1].astype(jnp.int32)


def draw_comp_kv(key, part):
    base = key_base(key)
    key = jax.random.fold_in(key, 3)
    values = jnp.clip(jax.random.normal(key, (PROMPTS, CTOK, DH), jnp.float32), -6.0, 6.0)
    return jnp.concatenate([base, values], -1).astype(jnp.bfloat16)


def draw_queries(key, part):
    key = jax.random.fold_in(key, 5)
    drawn = jnp.clip(jax.random.normal(key, (PROMPTS, CTOK, H * DH), jnp.float32), -6.0, 6.0)
    return drawn.astype(jnp.bfloat16)


def level_of(stream_key, shape, cuts, low, high):
    def one(axis_at, blocks):
        steps = jax.random.uniform(jax.random.fold_in(jax.random.fold_in(stream_key, 6), axis_at), (blocks,), jnp.float32, low / len(cuts), high / len(cuts))
        return jnp.repeat(jnp.exp(steps), shape[axis_at] // blocks).reshape((-1,) + (1,) * (len(shape) - axis_at - 1))

    level = one(*cuts[0])
    for cut in cuts[1:]:
        level = level * one(*cut)
    return level


def gaussian(rng, shape, spread, reach, shards=(), kind=jnp.bfloat16):
    loudness = level_of(rng, shape, shards, -0.22, 0.18) if shards else 1.0
    entries = jax.random.normal(rng, shape, jnp.float32) * spread * loudness
    return jnp.minimum(jnp.maximum(entries, -reach), reach).astype(kind)


def setup_inputs(seed: int = 0) -> dict:
    keys = jax.random.split(jax.random.key(seed), 8)
    queries = draw_queries(jax.random.fold_in(keys[7], 71), 0)
    comp_kv = draw_comp_kv(jax.random.fold_in(keys[7], 71), 0)
    out_grad = gaussian(keys[2], (PROMPTS, CTOK, H * DH), 1.0, 6.0, ((0, 4), (1, 64)))
    comp_ids = draw_comp_ids(jax.random.fold_in(keys[7], 71), 0)
    comp_pos = draw_comp_pos(jax.random.fold_in(keys[7], 71), 0)
    prompt_kv = gaussian(keys[5], (PROMPTS, PLEN, 2 * DH), 1.0, 6.0, ((0, 4), (1, 64)))
    owned_prompt = jax.random.permutation(keys[6], PROMPTS).astype(jnp.int32)
    return {"queries": queries, "comp_kv": comp_kv, "out_grad": out_grad, "comp_ids": comp_ids, "comp_pos": comp_pos, "prompt_kv": prompt_kv, "owned_prompt": owned_prompt}


def group_grads(queries, comp_kv, out_grad, comp_ids, comp_pos, prompt_kv):
    keys_all = jnp.concatenate([prompt_kv, comp_kv], 0).astype(jnp.float32)
    key_ids = jnp.concatenate([jnp.full((PLEN,), -1, jnp.int32), comp_ids.astype(jnp.int32)])
    key_pos = jnp.concatenate([jnp.full((PLEN,), -1, jnp.int32), comp_pos.astype(jnp.int32)])
    scale = 1.0 / math.sqrt(DH)
    nblocks = CTOK // TOK_DEV
    q_blocks = queries.reshape(nblocks, TOK_DEV, H, DH)
    d_blocks = out_grad.reshape(nblocks, TOK_DEV, H, DH)
    id_blocks = comp_ids.astype(jnp.int32).reshape(nblocks, TOK_DEV)
    pos_blocks = comp_pos.astype(jnp.int32).reshape(nblocks, TOK_DEV)

    def step(carry, inputs):
        qpart, dpart, idpart, pospart = inputs
        qfloat = qpart.astype(jnp.float32)
        dfloat = dpart.astype(jnp.float32)
        logits = jnp.einsum('thd,kd->thk', qfloat, keys_all[:, :DH]) * scale
        visible = (key_ids[None, :] == -1) | (key_ids[None, :] == idpart[:, None]) & (key_pos[None, :] <= pospart[:, None])
        logits = jnp.where(visible[:, None, :], logits, -1e+30)
        highest = lax.optimization_barrier(jnp.max(logits, -1, keepdims=True))
        lse = highest + jnp.log(lax.optimization_barrier(jnp.sum(jnp.exp(logits - highest), -1, keepdims=True)))
        probs = jnp.exp(logits - lse)
        dprobs = jnp.einsum('thd,kd->thk', dfloat, keys_all[:, DH:])
        delta = lax.optimization_barrier(jnp.sum(probs * dprobs, -1, keepdims=True))
        dlogits = probs * (dprobs - delta)
        probs_low = lax.optimization_barrier(probs.astype(jnp.bfloat16)).astype(jnp.float32)
        dlog_low = lax.optimization_barrier(dlogits.astype(jnp.bfloat16)).astype(jnp.float32)
        grad_q = jnp.einsum('thk,kd->thd', dlog_low, keys_all[:, :DH]) * scale
        grad_k = jnp.einsum('thk,thd->kd', dlog_low, qfloat) * scale
        grad_v = jnp.einsum('thk,thd->kd', probs_low, dfloat)
        newcarry = carry + jnp.concatenate([grad_k, grad_v], 1)
        return (newcarry, grad_q.astype(jnp.bfloat16).reshape(TOK_DEV, H * DH))
    start_sum = jnp.zeros((PLEN + CTOK, 2 * DH), jnp.float32)
    total, grad_q = lax.scan(step, start_sum, (q_blocks, d_blocks, id_blocks, pos_blocks))
    return (grad_q.reshape(CTOK, H * DH), total[PLEN:].astype(jnp.bfloat16), total[:PLEN].astype(jnp.bfloat16))

def reference(queries, comp_kv, out_grad, comp_ids, comp_pos, prompt_kv, owned_prompt):
    grad_queries = []
    grad_comp = []
    grad_prompt = []
    for group in range(PROMPTS):
        pick = (owned_prompt == group).astype(jnp.float32)
        mine = jnp.tensordot(pick, prompt_kv.astype(jnp.float32), 1).astype(jnp.bfloat16)
        gq, gc, gp = group_grads(queries[group], comp_kv[group], out_grad[group], comp_ids[group], comp_pos[group], mine)
        grad_queries.append(gq)
        grad_comp.append(gc)
        grad_prompt.append(gp)
    stacked = jnp.stack(grad_prompt).astype(jnp.float32)
    select = (owned_prompt[:, None] == jnp.arange(PROMPTS, dtype=jnp.int32)[None, :]).astype(jnp.float32)
    slotted = jnp.einsum('jg,grc->jrc', select, stacked).astype(jnp.bfloat16)
    return (jnp.stack(grad_queries), jnp.stack(grad_comp), slotted)
```

```python
import math

import jax
import jax.numpy as jnp
from jax import lax
from jax.experimental import pallas as pl
from jax.experimental.pallas import tpu as pltpu
from jax.sharding import PartitionSpec as P

XN = 4
ZN = 8
CN = 2
GN = 4
H = 5
DH = 128
TOK = 128
PTOK = 64
BLK = 32
SH = CN * ZN
ROWS = H * TOK
KT = 256
NPT = SH * PTOK // KT
NCT = SH * TOK // KT
NKB = SH * TOK // BLK
NQB = XN * TOK // BLK
BPT = KT // BLK
QPT = TOK // BLK
SPAN = 4096
SCALE = 1.0 / math.sqrt(DH)
LOG2E = 1.4426950408889634
C2 = SCALE * LOG2E
NEG = -1e30
MESH = pl.DeviceIdType.MESH
VM = 50 * 1024 * 1024


def place():
    s = lax.axis_index("seq")
    return s // (ZN * CN), lax.rem(s // CN, ZN), lax.rem(s, CN), lax.axis_index("grp")


def device(x, z, c, g):
    return (lax.rem(x + XN, XN) * (ZN * CN) + lax.rem(z + ZN, ZN) * CN + c, g)


class Copies:
    def __init__(self, send, recv):
        self.send, self.recv, self.n, self.all = send, recv, 0, []

    def start(self, src, dst, dev):
        cp = pltpu.make_async_remote_copy(
            src_ref=src,
            dst_ref=dst,
            send_sem=self.send.at[self.n],
            recv_sem=self.recv.at[self.n],
            device_id=dev,
            device_id_type=MESH,
        )
        self.n += 1
        cp.start()
        self.all.append(cp)
        return cp


def greet(devs):
    barrier = pltpu.get_barrier_semaphore()
    for dev in devs:
        pl.semaphore_signal(barrier, inc=1, device_id=dev, device_id_type=MESH)
    pl.semaphore_wait(barrier, len(devs))


N_GATHER = 96


def gather_kernel(q, d, kv, code, pkv, pick, gq, gd, gkv, gpk, gkc, gqc, slots, mine, send, recv, loc):
    x, z, c, g = place()
    xr, xl = device(x + 1, z, c, g), device(x - 1, z, c, g)
    zr, zl = device(x, z + 1, c, g), device(x, z - 1, c, g)
    peer = device(x, z, 1 - c, g)
    ys = [device(x, z, c, lax.rem(g + i, GN)) for i in range(1, GN)]
    greet([xr, xl, zr, zl, peer] + ys)
    cps = Copies(send, recv)
    own = c * ZN + z

    l_slot = pltpu.make_async_copy(pkv, slots.at[g], loc.at[0])
    l_slot.start()
    y_cps = [cps.start(pkv, slots.at[g], dev) for dev in ys]
    c_right = [cps.start(kv, gkv.at[own], zr), cps.start(code, gkc.at[own], zr)]
    c_left = [cps.start(kv, gkv.at[own], zl), cps.start(code, gkc.at[own], zl)]
    relays = [cps.start(kv, gkv.at[own], peer), cps.start(code, gkc.at[own], peer)]
    xq_r = cps.start(q, gq.at[x], xr)
    xd_l = cps.start(d, gd.at[x], xl)
    xq_l = cps.start(q, gq.at[x], xl)
    xd_r = cps.start(d, gd.at[x], xr)
    xc_r = cps.start(code, gqc.at[x], xr)
    xc_l = cps.start(code, gqc.at[x], xl)
    locs = [l_slot]
    for i, (a, b) in enumerate(((q, gq.at[x]), (d, gd.at[x]), (kv, gkv.at[own]), (code, gkc.at[own]), (code, gqc.at[x]))):
        cp = pltpu.make_async_copy(a, b, loc.at[i + 1])
        cp.start()
        locs.append(cp)

    l_slot.wait()
    for cp in y_cps:
        cp.wait_recv()
    total = jnp.zeros((PTOK, 2 * DH), jnp.float32)
    for j in range(GN):
        total = total + jnp.where(pick[j, 0:1, :] > 0.0, slots[j].astype(jnp.float32), 0.0)
    mine[...] = total.astype(jnp.bfloat16)
    l_mine = pltpu.make_async_copy(mine, gpk.at[own], loc.at[6])
    l_mine.start()
    locs.append(l_mine)
    p_right = [cps.start(mine, gpk.at[own], zr)]
    p_left = [cps.start(mine, gpk.at[own], zl)]
    relays.append(cps.start(mine, gpk.at[own], peer))

    half, phalf = TOK // 2, PTOK // 2
    x_fwd = []
    for t in range(1, 4):
        a = c * ZN + lax.rem(z - t + ZN, ZN)
        b = c * ZN + lax.rem(z + t, ZN)
        for cp in c_right:
            cp.wait_recv()
        if t < 3:
            c_right = [cps.start(gkv.at[a], gkv.at[a], zr), cps.start(gkc.at[a], gkc.at[a], zr)]
        else:
            c_right = [
                cps.start(gkv.at[a, pl.ds(0, half)], gkv.at[a, pl.ds(0, half)], zr),
                cps.start(gkc.at[a], gkc.at[a], zr),
            ]
        relays += [cps.start(gkv.at[a], gkv.at[a], peer), cps.start(gkc.at[a], gkc.at[a], peer)]
        for cp in c_left:
            cp.wait_recv()
        if t < 3:
            c_left = [cps.start(gkv.at[b], gkv.at[b], zl), cps.start(gkc.at[b], gkc.at[b], zl)]
        else:
            c_left = [cps.start(gkv.at[b, pl.ds(half, half)], gkv.at[b, pl.ds(half, half)], zl)]
        relays += [cps.start(gkv.at[b], gkv.at[b], peer), cps.start(gkc.at[b], gkc.at[b], peer)]
        for cp in p_right:
            cp.wait_recv()
        if t < 3:
            p_right = [cps.start(gpk.at[a], gpk.at[a], zr)]
        else:
            p_right = [cps.start(gpk.at[a, pl.ds(0, phalf)], gpk.at[a, pl.ds(0, phalf)], zr)]
        relays.append(cps.start(gpk.at[a], gpk.at[a], peer))
        for cp in p_left:
            cp.wait_recv()
        if t < 3:
            p_left = [cps.start(gpk.at[b], gpk.at[b], zl)]
        else:
            p_left = [cps.start(gpk.at[b, pl.ds(phalf, phalf)], gpk.at[b, pl.ds(phalf, phalf)], zl)]
        relays.append(cps.start(gpk.at[b], gpk.at[b], peer))
        if t == 2:
            xq_r.wait_recv()
            xl_i, xr_i = lax.rem(x - 1 + XN, XN), lax.rem(x + 1, XN)
            x_fwd.append(cps.start(gq.at[xl_i], gq.at[xl_i], xr))
            xc_r.wait_recv()
            x_fwd.append(cps.start(gqc.at[xl_i], gqc.at[xl_i], xr))
            xd_l.wait_recv()
            x_fwd.append(cps.start(gd.at[xr_i], gd.at[xr_i], xl))
    far = c * ZN + lax.rem(z + 4, ZN)
    for cp in c_right + c_left + p_right + p_left:
        cp.wait_recv()
    relays += [
        cps.start(gkv.at[far], gkv.at[far], peer),
        cps.start(gkc.at[far], gkc.at[far], peer),
        cps.start(gpk.at[far], gpk.at[far], peer),
    ]
    for cp in [xq_l, xd_r, xc_l] + x_fwd + relays:
        cp.wait_recv()
    for cp in locs[1:]:
        cp.wait()
    for cp in cps.all:
        cp.wait_send()


def gather(q, d, kv, code, pkv, pick):
    any_spec = pl.BlockSpec(memory_space=pl.ANY)
    vmem = pl.BlockSpec(memory_space=pltpu.VMEM)
    bf, i32 = jnp.bfloat16, jnp.int32
    return pl.pallas_call(
        gather_kernel,
        out_shape=[
            jax.ShapeDtypeStruct((XN, TOK, ROWS), bf),
            jax.ShapeDtypeStruct((XN, TOK, ROWS), bf),
            jax.ShapeDtypeStruct((SH, TOK, 2 * DH), bf),
            jax.ShapeDtypeStruct((SH, PTOK, 2 * DH), bf),
            jax.ShapeDtypeStruct((SH, 8, TOK), i32),
            jax.ShapeDtypeStruct((XN, 8, TOK), i32),
        ],
        in_specs=[any_spec] * 5 + [vmem],
        out_specs=[any_spec] * 6,
        scratch_shapes=[
            pltpu.VMEM((GN, PTOK, 2 * DH), bf),
            pltpu.VMEM((PTOK, 2 * DH), bf),
            pltpu.SemaphoreType.DMA((N_GATHER,)),
            pltpu.SemaphoreType.DMA((N_GATHER,)),
            pltpu.SemaphoreType.DMA((8,)),
        ],
        compiler_params=pltpu.CompilerParams(collective_id=0, has_side_effects=True, vmem_limit_bytes=VM),
    )(q, d, kv, code, pkv, pick)


def order(first, last):
    n = first.shape[0]
    at = jnp.arange(n, dtype=jnp.int32)
    rank = jnp.sum((first[None, :] < first[:, None]).astype(jnp.int32), 1)
    hit = rank[None, :] == at[:, None]
    pick = lambda v: jnp.sum(jnp.where(hit, v[None, :], 0), 1)
    return pick(at), pick(first), pick(last)


def plan(kcodes, qcodes):
    kblk = kcodes[:, 0, :].reshape(NKB, BLK)
    qblk = qcodes[:, 0, :].reshape(NQB, BLK)
    kperm, kfirst, _ = order(jnp.min(kblk, 1), jnp.max(kblk, 1))
    qperm, qfirst, qlast = order(jnp.min(qblk, 1), jnp.max(qblk, 1))
    seen = (kfirst[None, :] // SPAN == qfirst[:, None] // SPAN) & (kfirst[None, :] <= qlast[:, None])
    tiles = jnp.any(seen.reshape(XN, QPT, NCT, BPT), axis=(1, 3)).astype(jnp.int32)
    count = jnp.sum(tiles, 1)
    rank = jnp.cumsum(tiles, 1) - 1
    at = jnp.arange(NCT, dtype=jnp.int32)
    listed = jnp.sum(
        jnp.where((rank[:, None, :] == at[None, :, None]) & (tiles[:, None, :] > 0), at[None, None, :], 0), 2
    )
    return kperm, qperm, listed.reshape(-1), count


def nt(a, b):
    return lax.dot_general(a, b, (((1,), (1,)), ((), ())), preferred_element_type=jnp.float32)


def nn(a, b):
    return lax.dot_general(a, b, (((1,), (0,)), ((), ())), preferred_element_type=jnp.float32)


def tn(a, b):
    return lax.dot_general(a, b, (((0,), (0,)), ((), ())), preferred_element_type=jnp.float32)


def sort_tokens(qperm, gq, gd, qs, ds):
    def body(i, _):
        p = qperm[i]
        src, row = p // QPT, pl.multiple_of(lax.rem(p, QPT) * BLK, BLK)
        dst, off = i // QPT, pl.multiple_of(lax.rem(i, QPT) * BLK, BLK)
        for h in range(H):
            to = pl.ds(h * TOK + off, BLK)
            qs[dst, to, :] = gq[src, pl.ds(row, BLK), h * DH : (h + 1) * DH]
            ds[dst, to, :] = gd[src, pl.ds(row, BLK), h * DH : (h + 1) * DH]
        return 0

    lax.fori_loop(0, NQB, body, 0)


def sort_keys(kperm, gkv, gkc, skv, skc, wide):
    def widen(j, _):
        row = jnp.broadcast_to(gkc[j, 0:1, :], (TOK, TOK))
        wide[pl.ds(pl.multiple_of(j * TOK, TOK), TOK), :] = row.T
        return 0

    lax.fori_loop(0, SH, widen, 0)

    def body(i, _):
        p = kperm[i]
        to = pl.ds(pl.multiple_of(i * BLK, BLK), BLK)
        skv[to, :] = gkv[p // QPT, pl.ds(pl.multiple_of(lax.rem(p, QPT) * BLK, BLK), BLK), :]
        skc[to, :] = wide[pl.ds(pl.multiple_of(p * BLK, BLK), BLK), :]
        return 0

    lax.fori_loop(0, NKB, body, 0)


def visible(kc, qc):
    base = qc - jnp.bitwise_and(qc, SPAN - 1)
    mask = (kc <= qc) & (kc >= base)
    return jnp.concatenate([mask] * H, 1)


def stats_kernel(kperm, qperm, listed, count, gq, gd, gkv, gpk, gkc, sqc, out, qs, ds, skv, skc, wide):
    sort_tokens(qperm, gq, gd, qs, ds)
    sort_keys(kperm, gkv, gkc, skv, skc, wide)
    per = KT // PTOK

    def tile(qt, keys, mask, carry):
        m, l, w = carry
        s = nt(keys[:, :DH], qs[qt])
        if mask is not None:
            s = jnp.where(mask, s, NEG)
        dp = nt(keys[:, DH:], ds[qt])
        m2 = jnp.maximum(m, jnp.max(s, 0, keepdims=True) * C2)
        e = jnp.exp2(s * C2 - m2)
        a = jnp.exp2(m - m2)
        return m2, l * a + jnp.sum(e, 0, keepdims=True), w * a + jnp.sum(e * dp, 0, keepdims=True)

    def tokens(qt, _):
        def prompt(i, carry):
            return tile(qt, gpk[pl.ds(i * per, per)].reshape(KT, 2 * DH), None, carry)

        def comp(i, carry):
            kt = listed[qt * NCT + i]
            at = pl.ds(pl.multiple_of(kt * KT, KT), KT)
            return tile(qt, skv[at, :], visible(skc[at, :], sqc[qt, 0:1, :]), carry)

        carry = (jnp.full((1, ROWS), NEG, jnp.float32), jnp.zeros((1, ROWS), jnp.float32), jnp.zeros((1, ROWS), jnp.float32))
        carry = lax.fori_loop(0, NPT, prompt, carry)
        m, l, w = lax.fori_loop(0, count[qt], comp, carry)
        out[qt, 0:1, :] = m
        out[qt, 1:2, :] = l
        out[qt, 2:3, :] = w
        return 0

    lax.fori_loop(0, XN, tokens, 0)


SORT_SCRATCH = [
    pltpu.VMEM((XN, ROWS, DH), jnp.bfloat16),
    pltpu.VMEM((XN, ROWS, DH), jnp.bfloat16),
    pltpu.VMEM((SH * TOK, 2 * DH), jnp.bfloat16),
    pltpu.VMEM((SH * TOK, TOK), jnp.int32),
    pltpu.VMEM((SH * TOK, TOK), jnp.int32),
]


def stats(plans, gq, gd, gkv, gpk, gkc, sqc):
    vmem = pl.BlockSpec(memory_space=pltpu.VMEM)
    smem = pl.BlockSpec(memory_space=pltpu.SMEM)
    return pl.pallas_call(
        stats_kernel,
        out_shape=jax.ShapeDtypeStruct((XN, 8, ROWS), jnp.float32),
        in_specs=[smem] * 4 + [vmem] * 6,
        out_specs=vmem,
        scratch_shapes=SORT_SCRATCH,
        compiler_params=pltpu.CompilerParams(vmem_limit_bytes=VM),
    )(*plans, gq, gd, gkv, gpk, gkc, sqc)


def grads_kernel(
    kperm, qperm, listed, count, gq, gd, gkv, gpk, gkc, sqc, norm, dq_out, dkv_out, qs, ds, skv, skc, wide, dqt, dkp, dkc
):
    sort_tokens(qperm, gq, gd, qs, ds)
    sort_keys(kperm, gkv, gkc, skv, skc, wide)
    per = KT // PTOK
    dqt[...] = jnp.zeros_like(dqt)
    dkp[...] = jnp.zeros_like(dkp)
    dkc[...] = jnp.zeros_like(dkc)

    def tile(qt, keys, mask, acc, at):
        qrow, drow = qs[qt], ds[qt]
        lse, delta = norm[qt, 0:1, :], norm[qt, 1:2, :]
        k = keys[:, :DH]
        p = jnp.exp2(nt(k, qrow) * C2 - lse)
        if mask is not None:
            p = jnp.where(mask, p, 0.0)
        dl = (p * (nt(keys[:, DH:], drow) - delta)).astype(jnp.bfloat16)
        acc[at, :DH] += nn(dl, qrow)
        acc[at, DH:] += nn(p.astype(jnp.bfloat16), drow)
        dqt[qt] += tn(k, dl)

    def tokens(qt, _):
        def prompt(i, _):
            at = pl.ds(pl.multiple_of(i * KT, KT), KT)
            tile(qt, gpk[pl.ds(i * per, per)].reshape(KT, 2 * DH), None, dkp, at)
            return 0

        def comp(i, _):
            kt = listed[qt * NCT + i]
            at = pl.ds(pl.multiple_of(kt * KT, KT), KT)
            tile(qt, skv[at, :], visible(skc[at, :], sqc[qt, 0:1, :]), dkc, at)
            return 0

        lax.fori_loop(0, NPT, prompt, 0)
        lax.fori_loop(0, count[qt], comp, 0)
        return 0

    lax.fori_loop(0, XN, tokens, 0)

    def put_prompt(j, _):
        at = pl.ds(pl.multiple_of(j * PTOK, PTOK), PTOK)
        dkv_out[j, 0:PTOK, :DH] = (dkp[at, :DH] * SCALE).astype(jnp.bfloat16)
        dkv_out[j, 0:PTOK, DH:] = dkp[at, DH:].astype(jnp.bfloat16)
        return 0

    lax.fori_loop(0, SH, put_prompt, 0)

    def put_comp(i, _):
        p = kperm[i]
        at = pl.ds(pl.multiple_of(i * BLK, BLK), BLK)
        to = pl.ds(pl.multiple_of(PTOK + lax.rem(p, QPT) * BLK, BLK), BLK)
        dkv_out[p // QPT, to, :DH] = (dkc[at, :DH] * SCALE).astype(jnp.bfloat16)
        dkv_out[p // QPT, to, DH:] = dkc[at, DH:].astype(jnp.bfloat16)
        return 0

    lax.fori_loop(0, NKB, put_comp, 0)

    def put_query(qt, _):
        for h in range(H):
            part = (dqt[qt, :, h * TOK : (h + 1) * TOK].T * SCALE).astype(jnp.bfloat16)
            for b in range(QPT):
                p = qperm[qt * QPT + b]
                to = pl.ds(pl.multiple_of(lax.rem(p, QPT) * BLK, BLK), BLK)
                dq_out[p // QPT, to, h * DH : (h + 1) * DH] = part[b * BLK : (b + 1) * BLK]
        return 0

    lax.fori_loop(0, XN, put_query, 0)


def grads(plans, gq, gd, gkv, gpk, gkc, sqc, norm):
    vmem = pl.BlockSpec(memory_space=pltpu.VMEM)
    smem = pl.BlockSpec(memory_space=pltpu.SMEM)
    return pl.pallas_call(
        grads_kernel,
        out_shape=[
            jax.ShapeDtypeStruct((XN, TOK, ROWS), jnp.bfloat16),
            jax.ShapeDtypeStruct((SH, PTOK + TOK, 2 * DH), jnp.bfloat16),
        ],
        in_specs=[smem] * 4 + [vmem] * 7,
        out_specs=[vmem] * 2,
        scratch_shapes=SORT_SCRATCH
        + [
            pltpu.VMEM((XN, DH, ROWS), jnp.float32),
            pltpu.VMEM((SH * PTOK, 2 * DH), jnp.float32),
            pltpu.VMEM((SH * TOK, 2 * DH), jnp.float32),
        ],
        compiler_params=pltpu.CompilerParams(vmem_limit_bytes=VM),
    )(*plans, gq, gd, gkv, gpk, gkc, sqc, norm)


def merge_kernel(part, out, buf, send, recv):
    x, z, c, g = place()
    xs = [device(x + i, z, c, g) for i in range(1, XN)]
    greet(xs)
    cps = Copies(send, recv)
    buf[x] = part[...]
    for dev in xs:
        cps.start(part, buf.at[x], dev)
    for cp in cps.all:
        cp.wait_recv()
    m = buf[0, :, 0:1, :]
    for i in range(1, XN):
        m = jnp.maximum(m, buf[i, :, 0:1, :])
    l = jnp.zeros_like(m)
    w = jnp.zeros_like(m)
    for i in range(XN):
        a = jnp.exp2(buf[i, :, 0:1, :] - m)
        l = l + buf[i, :, 1:2, :] * a
        w = w + buf[i, :, 2:3, :] * a
    out[:, 0:1, :] = m + jnp.log2(l)
    out[:, 1:2, :] = w / l
    for cp in cps.all:
        cp.wait_send()


def merge(part):
    vmem = pl.BlockSpec(memory_space=pltpu.VMEM)
    return pl.pallas_call(
        merge_kernel,
        out_shape=jax.ShapeDtypeStruct((XN, 8, ROWS), jnp.float32),
        in_specs=[vmem],
        out_specs=vmem,
        scratch_shapes=[
            pltpu.VMEM((XN, XN, 8, ROWS), jnp.float32),
            pltpu.SemaphoreType.DMA((3,)),
            pltpu.SemaphoreType.DMA((3,)),
        ],
        compiler_params=pltpu.CompilerParams(collective_id=1, has_side_effects=True, vmem_limit_bytes=VM),
    )(part)


N_REDUCE = 24
RW = PTOK + TOK


def reduce_kernel(dq, dkv, pick, dq_out, dkv_out, dp_out, qbuf, cbuf, rbuf, lbuf, sbuf, tbuf, mine, slots, send, recv):
    x, z, c, g = place()
    xs = [device(x + i, z, c, g) for i in range(1, XN)]
    zr, zl = device(x, z + 1, c, g), device(x, z - 1, c, g)
    peer = device(x, z, 1 - c, g)
    ys = [device(x, z, c, lax.rem(g + i, GN)) for i in range(1, GN)]
    greet(xs + [zr, zl, peer] + ys)
    cps = Copies(send, recv)
    f32, bf = jnp.float32, jnp.bfloat16
    pair = cps.start(dkv.at[pl.ds((1 - c) * ZN, ZN)], cbuf, peer)
    q_cps = [cps.start(dq.at[lax.rem(x + i, XN)], qbuf.at[x], xs[i - 1]) for i in range(1, XN)]
    pair.wait_recv()

    def own(owner):
        at = lax.rem(owner + ZN, ZN)
        return dkv[c * ZN + at].astype(f32) + cbuf[at].astype(f32)

    half = RW // 2
    far = own(z + 4)
    sbuf[0, 0:half, :] = far[:half].astype(bf)
    tbuf[0, half:, :] = far[half:].astype(bf)
    up = cps.start(sbuf.at[0, pl.ds(0, half)], rbuf.at[0, pl.ds(0, half)], zr)
    down = cps.start(tbuf.at[0, pl.ds(half, half)], lbuf.at[0, pl.ds(half, half)], zl)
    for t in range(1, 4):
        a, b = own(z + 4 - t), own(z - 4 + t)
        up.wait_recv()
        if t == 1:
            sbuf[t, 0:half, :] = (a[:half] + rbuf[0, 0:half, :].astype(f32)).astype(bf)
            sbuf[t, half:, :] = a[half:].astype(bf)
        else:
            sbuf[t] = (a + rbuf[t - 1].astype(f32)).astype(bf)
        up = cps.start(sbuf.at[t], rbuf.at[t], zr)
        down.wait_recv()
        if t == 1:
            tbuf[t, 0:half, :] = b[:half].astype(bf)
            tbuf[t, half:, :] = (b[half:] + lbuf[0, half:, :].astype(f32)).astype(bf)
        else:
            tbuf[t] = (b + lbuf[t - 1].astype(f32)).astype(bf)
        down = cps.start(tbuf.at[t], lbuf.at[t], zl)
    last = own(z)
    up.wait_recv()
    down.wait_recv()
    last = (last + rbuf[3].astype(f32) + lbuf[3].astype(f32)).astype(bf)
    mine[...] = last[:PTOK]
    y_cps = [cps.start(mine, slots.at[g], dev) for dev in ys]
    slots[g] = last[:PTOK]
    dkv_out[...] = last[PTOK:]
    for cp in q_cps:
        cp.wait_recv()
    qbuf[x] = dq[x]
    tot = qbuf[0].astype(f32)
    for i in range(1, XN):
        tot = tot + qbuf[i].astype(f32)
    dq_out[...] = tot.astype(bf)
    for cp in y_cps:
        cp.wait_recv()
    tot = jnp.zeros((PTOK, 2 * DH), f32)
    for j in range(GN):
        tot = tot + jnp.where(pick[j, 0:1, :] > 0.0, slots[j].astype(f32), 0.0)
    dp_out[...] = tot.astype(bf)
    for cp in cps.all:
        cp.wait_send()


def reduce(dq, dkv, pick):
    vmem = pl.BlockSpec(memory_space=pltpu.VMEM)
    bf = jnp.bfloat16
    return pl.pallas_call(
        reduce_kernel,
        out_shape=[
            jax.ShapeDtypeStruct((TOK, ROWS), bf),
            jax.ShapeDtypeStruct((TOK, 2 * DH), bf),
            jax.ShapeDtypeStruct((PTOK, 2 * DH), bf),
        ],
        in_specs=[vmem] * 3,
        out_specs=[vmem] * 3,
        scratch_shapes=[
            pltpu.VMEM((XN, TOK, ROWS), bf),
            pltpu.VMEM((ZN, RW, 2 * DH), bf),
            pltpu.VMEM((4, RW, 2 * DH), bf),
            pltpu.VMEM((4, RW, 2 * DH), bf),
            pltpu.VMEM((4, RW, 2 * DH), bf),
            pltpu.VMEM((4, RW, 2 * DH), bf),
            pltpu.VMEM((PTOK, 2 * DH), bf),
            pltpu.VMEM((GN, PTOK, 2 * DH), bf),
            pltpu.SemaphoreType.DMA((N_REDUCE,)),
            pltpu.SemaphoreType.DMA((N_REDUCE,)),
        ],
        compiler_params=pltpu.CompilerParams(collective_id=2, has_side_effects=True, vmem_limit_bytes=VM),
    )(dq, dkv, pick)


def shards(queries, comp_kv, out_grad, comp_ids, comp_pos, prompt_kv, owned_prompt):
    group = lax.axis_index("grp")
    code = jnp.broadcast_to(comp_ids * SPAN + comp_pos, (8, TOK))
    mine_in = jnp.broadcast_to((owned_prompt == group).astype(jnp.float32)[:, None, None], (GN, 8, 2 * DH))
    slot = jnp.arange(GN, dtype=jnp.int32)
    mine_out = jnp.broadcast_to((slot == owned_prompt[group]).astype(jnp.float32)[:, None, None], (GN, 8, 2 * DH))
    gq, gd, gkv, gpk, gkc, gqc = gather(queries[0], out_grad[0], comp_kv[0], code, prompt_kv[0], mine_in)
    plans = plan(gkc, gqc)
    sqc = gqc[:, 0, :].reshape(NQB, BLK)[plans[1]].reshape(XN, 1, TOK)
    sqc = jnp.broadcast_to(sqc, (XN, 8, TOK))
    part = stats(plans, gq, gd, gkv, gpk, gkc, sqc)
    norm = merge(part)
    dq, dkv = grads(plans, gq, gd, gkv, gpk, gkc, sqc, norm)
    grad_q, grad_c, grad_p = reduce(dq, dkv, mine_out)
    return grad_q[None], grad_c[None], grad_p[None]


def solution(mesh):
    placed = (
        P("grp", "seq", None),
        P("grp", "seq", None),
        P("grp", "seq", None),
        P("grp", "seq"),
        P("grp", "seq"),
        P("grp", "seq", None),
        P(),
    )
    return jax.shard_map(
        shards,
        mesh=mesh,
        in_specs=placed,
        out_specs=(P("grp", "seq", None), P("grp", "seq", None), P("grp", "seq", None)),
        check_vma=False,
    )
```

```python
import math

import jax
import jax.numpy as jnp
from jax import lax
from jax.experimental import pallas as pl
from jax.experimental.pallas import tpu as pltpu
from jax.sharding import PartitionSpec as P

XN = 4
ZN = 8
CN = 2
GN = 4
H = 5
DH = 128
TOK = 128
PTOK = 64
ROWS = H * TOK
UNIT = 512
SPAN = 4096
SCALE = 1.0 / math.sqrt(DH)
C2 = SCALE * 1.4426950408889634
NEG = -1e30
MESH = pl.DeviceIdType.MESH
N_SEM = 112

COMP_AT = [1, 7, 2, 6, 3, 5, 4, 0]
PROMPT_AT = [0, 1, 7, 2, 6, 3, 5, 4]


def comp_slot(o):
    at = COMP_AT.index(o)
    return at // 2, (at % 2) * CN * TOK


def prompt_slot(o):
    at = PROMPT_AT.index(o)
    return 4 + at // 4, (at % 4) * CN * PTOK


def nt(a, b):
    return lax.dot_general(a, b, (((1,), (1,)), ((), ())), preferred_element_type=jnp.float32)


def nn(a, b):
    return lax.dot_general(a, b, (((1,), (0,)), ((), ())), preferred_element_type=jnp.float32)


def tn(a, b):
    return lax.dot_general(a, b, (((0,), (0,)), ((), ())), preferred_element_type=jnp.float32)


def kernel(
    owned,
    ids,
    pos,
    q_in,
    d_in,
    kv_in,
    p_in,
    dq_out,
    dc_out,
    dp_out,
    code,
    gq,
    gd,
    gqc,
    gkc,
    keys,
    wide,
    qs,
    ds,
    slots,
    mine,
    st,
    sbuf,
    norm,
    acc,
    dqt,
    own_c,
    own_p,
    pair_s,
    pair_r,
    zs,
    zin_c,
    zin_p,
    dqs,
    dqr,
    yslots,
    send,
    recv,
    loc,
):
    f32, bf = jnp.float32, jnp.bfloat16
    s_at = lax.axis_index("seq")
    g = lax.axis_index("grp")
    x, z, c = s_at // (ZN * CN), lax.rem(s_at // CN, ZN), lax.rem(s_at, CN)

    def dev(dx, dz, dc, dg=0):
        xx, zz, gg = lax.rem(x + dx, XN), lax.rem(z + dz, ZN), lax.rem(g + dg, GN)
        cc = 1 - c if dc else c
        return (xx * (ZN * CN) + zz * CN + cc, gg)

    everyone = []
    count = [0]

    def start(src, dst, to):
        cp = pltpu.make_async_remote_copy(
            src_ref=src,
            dst_ref=dst,
            send_sem=send.at[count[0]],
            recv_sem=recv.at[count[0]],
            device_id=to,
            device_id_type=MESH,
        )
        count[0] += 1
        cp.start()
        everyone.append(cp)
        return cp

    def got(*cps):
        for cp in cps:
            cp.wait_recv()

    local_n = [0]

    def local(src, dst):
        cp = pltpu.make_async_copy(src, dst, loc.at[local_n[0]])
        local_n[0] += 1
        cp.start()
        return cp

    def comp_rows(o, other, lo=0, n=TOK):
        u, r = comp_slot(o)
        return keys.at[u, pl.ds(r + other * TOK + lo, n)]

    def prompt_rows(o, other, lo=0, n=PTOK):
        u, r = prompt_slot(o)
        return keys.at[u, pl.ds(r + other * PTOK + lo, n)]

    def code_row(o, other):
        u, r = comp_slot(o)
        return gkc.at[u * 4 + r // TOK + other]

    l_q = local(q_in, gq.at[0])
    l_d = local(d_in, gd.at[0])
    l_kv = local(kv_in, comp_rows(0, 0))
    l_p = local(p_in, slots.at[0])
    code[...] = jnp.broadcast_to(ids[...] * SPAN + pos[...], (8, TOK))
    gqc[0] = code[...]
    u0, r0 = comp_slot(0)
    gkc[u0 * 4 + r0 // TOK] = code[...]

    peer = dev(0, 0, 1)
    barrier = pltpu.get_barrier_semaphore()
    friends = [dev(i, 0, 0) for i in range(1, XN)] + [dev(0, 0, 0, i) for i in range(1, GN)]
    friends += [dev(0, i, 0) for i in range(1, ZN)] + [dev(0, i, 1) for i in range(ZN)]
    for to in friends:
        pl.semaphore_signal(barrier, inc=1, device_id=to, device_id_type=MESH)
    pl.semaphore_wait(barrier, len(friends))

    y_cps = [start(p_in, slots.at[GN - i], dev(0, 0, 0, i)) for i in range(1, GN)]
    k_cps = {}
    r_cps = {0: start(kv_in, comp_rows(0, 1), peer)}
    for i in (1, 7):
        k_cps[8 - i] = start(kv_in, comp_rows(8 - i, 0), dev(0, i, 0))
    xq, xd = {}, {}
    for i in (1, 3):
        xq[XN - i] = start(q_in, gq.at[XN - i], dev(i, 0, 0))
        xd[XN - i] = start(d_in, gd.at[XN - i], dev(i, 0, 0))
    for i in (2, 6):
        k_cps[8 - i] = start(kv_in, comp_rows(8 - i, 0), dev(0, i, 0))
    code_cps = [start(code, code_row(0, 1), peer)]
    for i in range(1, ZN):
        code_cps.append(start(code, code_row(ZN - i, 0), dev(0, i, 0)))
        code_cps.append(start(code, code_row(ZN - i, 1), dev(0, i, 1)))
    for i in range(1, XN):
        code_cps.append(start(code, gqc.at[XN - i], dev(i, 0, 0)))

    for i in range(XN):
        st[i, 0:1, :] = jnp.full((1, ROWS), NEG, f32)
        st[i, 1:2, :] = jnp.zeros((1, ROWS), f32)
        st[i, 2:3, :] = jnp.zeros((1, ROWS), f32)

    def spread(i):
        for h in range(H):
            qs[i, h * TOK : (h + 1) * TOK, :] = gq[i, :, h * DH : (h + 1) * DH]
            ds[i, h * TOK : (h + 1) * TOK, :] = gd[i, :, h * DH : (h + 1) * DH]

    def visible(u, i):
        qc = gqc[i, 0:1, :]
        kc = wide[u]
        base = qc - jnp.bitwise_and(qc, SPAN - 1)
        return jnp.concatenate([(kc <= qc) & (kc >= base)] * H, 1)

    def stat_tile(u, i, masked):
        k = keys[u]
        s = nt(k[:, :DH], qs[i])
        if masked:
            s = jnp.where(visible(u, i), s, NEG)
        dp = nt(k[:, DH:], ds[i])
        m = st[i, 0:1, :]
        m2 = jnp.maximum(m, jnp.max(s, 0, keepdims=True) * C2)
        e = jnp.exp2(s * C2 - m2)
        a = jnp.exp2(m - m2)
        st[i, 0:1, :] = m2
        st[i, 1:2, :] = st[i, 1:2, :] * a + jnp.sum(e, 0, keepdims=True)
        st[i, 2:3, :] = st[i, 2:3, :] * a + jnp.sum(e * dp, 0, keepdims=True)

    def loop(n, body):
        def step(j, _):
            body(j)
            return 0

        lax.fori_loop(0, n, step, 0)

    l_p.wait()
    got(*y_cps)
    total = jnp.zeros((PTOK, 2 * DH), f32)
    for i in range(GN):
        w = (owned[lax.rem(g + i, GN)] == g).astype(f32)
        total = total + slots[i].astype(f32) * w
    mine[...] = total.astype(bf)
    p_cps = {}
    rp_cps = {0: start(mine, prompt_rows(0, 1), peer)}
    for i in (1, 7, 2, 6):
        p_cps[8 - i] = start(mine, prompt_rows(8 - i, 0), dev(0, i, 0))
    u, r = prompt_slot(0)
    keys[u, r : r + PTOK, :] = mine[...]

    def relay(o):
        r_cps[o] = start(comp_rows(o, 0), comp_rows(o, 1), peer)

    def relay_p(o):
        rp_cps[o] = start(prompt_rows(o, 0), prompt_rows(o, 1), peer)

    got(k_cps[1], k_cps[7])
    relay(1)
    relay(7)
    got(*code_cps)

    def widen(j):
        wide[j // 4, pl.ds(pl.multiple_of(lax.rem(j, 4) * TOK, TOK), TOK), :] = jnp.broadcast_to(
            gkc[j, 0:1, :], (TOK, TOK)
        ).T

    loop(4 * 4, widen)
    l_q.wait()
    l_d.wait()
    l_kv.wait()
    spread(0)
    got(k_cps[2], k_cps[6])
    relay(2)
    relay(6)
    half, phalf = TOK // 2, PTOK // 2
    k_cps[5] = start(comp_rows(6, 0), comp_rows(5, 0), dev(0, 1, 0))
    k_cps[3] = start(comp_rows(2, 0), comp_rows(3, 0), dev(0, 7, 0))
    far = [
        start(comp_rows(6, 0, 0, half), comp_rows(4, 0, 0, half), dev(0, 2, 0)),
        start(comp_rows(2, 0, half, half), comp_rows(4, 0, half, half), dev(0, 6, 0)),
    ]
    got(r_cps[1], r_cps[7])
    stat_tile(0, 0, True)
    got(p_cps[1], p_cps[7], p_cps[2], p_cps[6])
    p_cps[5] = start(prompt_rows(6, 0), prompt_rows(5, 0), dev(0, 1, 0))
    p_cps[3] = start(prompt_rows(2, 0), prompt_rows(3, 0), dev(0, 7, 0))
    pfar = [
        start(prompt_rows(6, 0, 0, phalf), prompt_rows(4, 0, 0, phalf), dev(0, 2, 0)),
        start(prompt_rows(2, 0, phalf, phalf), prompt_rows(4, 0, phalf, phalf), dev(0, 6, 0)),
    ]
    for o in (1, 7, 2, 6):
        relay_p(o)
    got(xq[3], xd[3], xq[1], xd[1])
    xq[2] = start(gq.at[3], gq.at[2], dev(1, 0, 0))
    xd[2] = start(gd.at[1], gd.at[2], dev(3, 0, 0))
    spread(1)
    spread(3)
    got(r_cps[2], r_cps[6])
    stat_tile(1, 0, True)
    loop(4, lambda j: stat_tile(j // 2, 1 + 2 * lax.rem(j, 2), True))
    got(k_cps[3], k_cps[5], *far)
    for o in (3, 5, 4):
        relay(o)
    got(p_cps[3], p_cps[5], *pfar)
    for o in (3, 5, 4):
        relay_p(o)
    got(rp_cps[0], rp_cps[1], rp_cps[7], rp_cps[2])
    loop(3, lambda j: stat_tile(4, j + j // 2, False))
    got(r_cps[0], r_cps[3], r_cps[5], r_cps[4])
    loop(6, lambda j: stat_tile(2 + j // 3, lax.rem(j, 3) + lax.rem(j, 3) // 2, True))
    got(rp_cps[6], rp_cps[3], rp_cps[5], rp_cps[4])
    loop(3, lambda j: stat_tile(5, j + j // 2, False))
    st_cps = []

    def share(i):
        for j in range(1, XN):
            st_cps.append(start(st.at[i], sbuf.at[XN - 1 - j, (i - j) % XN], dev(j, 0, 0)))

    for i in (0, 1, 3):
        share(i)
    got(xq[2], xd[2])
    spread(2)
    loop(4, lambda u: stat_tile(u, 2, True))
    loop(2, lambda u: stat_tile(4 + u, 2, False))
    share(2)
    dqt[...] = jnp.zeros_like(dqt)
    acc[...] = jnp.zeros_like(acc)
    got(*st_cps)
    for i in range(XN):
        parts = [st[i]] + [sbuf[j, i] for j in range(XN - 1)]
        m = parts[0][0:1]
        for p in parts[1:]:
            m = jnp.maximum(m, p[0:1])
        l = jnp.zeros_like(m)
        w = jnp.zeros_like(m)
        for p in parts:
            a = jnp.exp2(p[0:1] - m)
            l = l + p[1:2] * a
            w = w + p[2:3] * a
        norm[i, 0:1, :] = m + jnp.log2(l)
        norm[i, 1:2, :] = w / l

    def grad_tile(u, i, masked, a):
        kk = keys[u]
        k = kk[:, :DH]
        qrow, drow = qs[i], ds[i]
        p = jnp.exp2(nt(k, qrow) * C2 - norm[i, 0:1, :])
        if masked:
            p = jnp.where(visible(u, i), p, 0.0)
        dl = (p * (nt(kk[:, DH:], drow) - norm[i, 1:2, :])).astype(bf)
        acc[a, :, :DH] += nn(dl, qrow)
        acc[a, :, DH:] += nn(p.astype(bf), drow)
        dqt[i] += tn(k, dl)

    pair_cps, z_cps = {}, {}

    def emit(u, a, own, n, first):
        for t in range(UNIT // (2 * n)):
            r = t * 2 * n
            own[first + t, :, :DH] = acc[a, r : r + n, :DH] * SCALE
            own[first + t, :, DH:] = acc[a, r : r + n, DH:]
            pair_s[u, t * n : (t + 1) * n, :DH] = (acc[a, r + n : r + 2 * n, :DH] * SCALE).astype(bf)
            pair_s[u, t * n : (t + 1) * n, DH:] = acc[a, r + n : r + 2 * n, DH:].astype(bf)
        pair_cps[u] = start(pair_s.at[u], pair_r.at[u], peer)

    def forward(u, own, n, first, at, zin):
        got(pair_cps[u])
        for t in range(UNIT // (2 * n)):
            o = at[first + t]
            both = own[first + t] + pair_r[u, t * n : (t + 1) * n, :].astype(f32)
            if o == 0:
                own[first + t] = both
            else:
                zs[u, t * n : (t + 1) * n, :] = both.astype(bf)
                z_cps[(u, o)] = start(zs.at[u, pl.ds(t * n, n)], zin.at[ZN - 1 - o], dev(0, o, 0))

    loop(4, lambda i: grad_tile(5, i, False, 0))
    emit(5, 0, own_p, PTOK, 4)
    acc[0] = jnp.zeros_like(acc[0])
    loop(4, lambda i: grad_tile(4, i, False, 0))
    emit(4, 0, own_p, PTOK, 0)
    acc[0] = jnp.zeros_like(acc[0])
    forward(5, own_p, PTOK, 4, PROMPT_AT, zin_p)
    loop(4, lambda i: grad_tile(2, i, True, 0))
    emit(2, 0, own_c, TOK, 4)
    acc[0] = jnp.zeros_like(acc[0])
    forward(4, own_p, PTOK, 0, PROMPT_AT, zin_p)
    loop(4, lambda i: grad_tile(1, i, True, 0))
    emit(1, 0, own_c, TOK, 2)
    acc[0] = jnp.zeros_like(acc[0])
    forward(2, own_c, TOK, 4, COMP_AT, zin_c)

    def put_query(i):
        for h in range(H):
            part = dqt[i, :, h * TOK : (h + 1) * TOK].T * SCALE
            dqs[i, :, h * DH : (h + 1) * DH] = part.astype(bf)

    dq_cps = []
    my_cps = []
    for n, i in enumerate((2, 1, 3, 0)):
        loop(2, lambda j: grad_tile(3 * j, i, True, j))
        put_query(i)
        if i:
            dq_cps.append(start(dqs.at[i], dqr.at[XN - 1 - i], dev(i, 0, 0)))
        if n == 0:
            forward(1, own_c, TOK, 2, COMP_AT, zin_c)
        if n == 2:
            got(*[cp for (u, o), cp in z_cps.items() if u >= 4])
            total = own_p[0]
            for j in range(ZN - 1):
                total = total + zin_p[j].astype(f32)
            yslots[0] = total.astype(bf)
            my_cps = [start(yslots.at[0], yslots.at[GN - j], dev(0, 0, 0, j)) for j in range(1, GN)]
    emit(0, 0, own_c, TOK, 0)
    emit(3, 1, own_c, TOK, 6)
    forward(0, own_c, TOK, 0, COMP_AT, zin_c)
    forward(3, own_c, TOK, 6, COMP_AT, zin_c)
    got(*my_cps)
    total = jnp.zeros((PTOK, 2 * DH), f32)
    wanted = owned[g]
    for i in range(GN):
        w = (wanted == lax.rem(g + i, GN)).astype(f32)
        total = total + yslots[i].astype(f32) * w
    dp_out[...] = total.astype(bf)
    got(*dq_cps)
    total = dqs[0].astype(f32)
    for j in range(XN - 1):
        total = total + dqr[j].astype(f32)
    dq_out[...] = total.astype(bf)
    got(*[cp for (u, o), cp in z_cps.items() if u < 4])
    total = own_c[COMP_AT.index(0)]
    for j in range(ZN - 1):
        total = total + zin_c[j].astype(f32)
    dc_out[...] = total.astype(bf)
    for cp in everyone:
        cp.wait_send()


def shards(queries, comp_kv, out_grad, comp_ids, comp_pos, prompt_kv, owned_prompt):
    bf, f32, i32 = jnp.bfloat16, jnp.float32, jnp.int32
    hbm = pl.BlockSpec(memory_space=pl.ANY)
    vmem = pl.BlockSpec(memory_space=pltpu.VMEM)
    smem = pl.BlockSpec(memory_space=pltpu.SMEM)
    grad_q, grad_c, grad_p = pl.pallas_call(
        kernel,
        out_shape=[
            jax.ShapeDtypeStruct((TOK, ROWS), bf),
            jax.ShapeDtypeStruct((TOK, 2 * DH), bf),
            jax.ShapeDtypeStruct((PTOK, 2 * DH), bf),
        ],
        in_specs=[smem, vmem, vmem] + [hbm] * 4,
        out_specs=[vmem] * 3,
        scratch_shapes=[
            pltpu.VMEM((8, TOK), i32),
            pltpu.VMEM((XN, TOK, ROWS), bf),
            pltpu.VMEM((XN, TOK, ROWS), bf),
            pltpu.VMEM((XN, 8, TOK), i32),
            pltpu.VMEM((16, 8, TOK), i32),
            pltpu.VMEM((6, UNIT, 2 * DH), bf),
            pltpu.VMEM((4, UNIT, TOK), i32),
            pltpu.VMEM((XN, ROWS, DH), bf),
            pltpu.VMEM((XN, ROWS, DH), bf),
            pltpu.VMEM((GN, PTOK, 2 * DH), bf),
            pltpu.VMEM((PTOK, 2 * DH), bf),
            pltpu.VMEM((XN, 8, ROWS), f32),
            pltpu.VMEM((XN - 1, XN, 8, ROWS), f32),
            pltpu.VMEM((XN, 8, ROWS), f32),
            pltpu.VMEM((2, UNIT, 2 * DH), f32),
            pltpu.VMEM((XN, DH, ROWS), f32),
            pltpu.VMEM((ZN, TOK, 2 * DH), f32),
            pltpu.VMEM((ZN, PTOK, 2 * DH), f32),
            pltpu.VMEM((6, UNIT // 2, 2 * DH), bf),
            pltpu.VMEM((6, UNIT // 2, 2 * DH), bf),
            pltpu.VMEM((6, UNIT // 2, 2 * DH), bf),
            pltpu.VMEM((ZN - 1, TOK, 2 * DH), bf),
            pltpu.VMEM((ZN - 1, PTOK, 2 * DH), bf),
            pltpu.VMEM((XN, TOK, ROWS), bf),
            pltpu.VMEM((XN - 1, TOK, ROWS), bf),
            pltpu.VMEM((GN, PTOK, 2 * DH), bf),
            pltpu.SemaphoreType.DMA((N_SEM,)),
            pltpu.SemaphoreType.DMA((N_SEM,)),
            pltpu.SemaphoreType.DMA((4,)),
        ],
        compiler_params=pltpu.CompilerParams(
            collective_id=0, has_side_effects=True, vmem_limit_bytes=60 * 1024 * 1024
        ),
    )(owned_prompt, comp_ids, comp_pos, queries[0], out_grad[0], comp_kv[0], prompt_kv[0])
    return grad_q[None], grad_c[None], grad_p[None]


def solution(mesh):
    placed = (
        P("grp", "seq", None),
        P("grp", "seq", None),
        P("grp", "seq", None),
        P("grp", "seq"),
        P("grp", "seq"),
        P("grp", "seq", None),
        P(),
    )
    return jax.shard_map(
        shards,
        mesh=mesh,
        in_specs=placed,
        out_specs=(P("grp", "seq", None), P("grp", "seq", None), P("grp", "seq", None)),
        check_vma=False,
    )
```

```python
import math

import jax
import jax.numpy as jnp
from jax import lax
from jax.experimental import pallas as pl
from jax.experimental.pallas import tpu as pltpu
from jax.sharding import PartitionSpec as P

XN = 4
ZN = 8
CN = 2
GN = 4
H = 5
DH = 128
TOK = 128
PTOK = 64
ROWS = H * TOK
UNIT = 512
SPAN = 4096
SCALE = 1.0 / math.sqrt(DH)
C2 = SCALE * 1.4426950408889634
NEG = -1e30
MESH = pl.DeviceIdType.MESH
N_SEM = 112

COMP_AT = [1, 7, 2, 6, 3, 5, 4, 0]
PROMPT_AT = [0, 1, 7, 2, 6, 3, 5, 4]
PAIRS = [(1, 3), (0, 2)]
WIDE = 2 * ROWS


def token_slot(i):
    for p, pair in enumerate(PAIRS):
        if i in pair:
            return p, pair.index(i) * ROWS


def comp_slot(o):
    at = COMP_AT.index(o)
    return at // 2, (at % 2) * CN * TOK


def prompt_slot(o):
    at = PROMPT_AT.index(o)
    return 4 + at // 4, (at % 4) * CN * PTOK


def nt(a, b):
    return lax.dot_general(a, b, (((1,), (1,)), ((), ())), preferred_element_type=jnp.float32)


def nn(a, b):
    return lax.dot_general(a, b, (((1,), (0,)), ((), ())), preferred_element_type=jnp.float32)


def tn(a, b):
    return lax.dot_general(a, b, (((0,), (0,)), ((), ())), preferred_element_type=jnp.float32)


def kernel(
    owned,
    ids,
    pos,
    q_in,
    d_in,
    kv_in,
    p_in,
    dq_out,
    dc_out,
    dp_out,
    code,
    gq,
    gd,
    gqc,
    gkc,
    keys,
    wide,
    qs,
    ds,
    slots,
    mine,
    st,
    sbuf,
    norm,
    logit,
    acc,
    dqt,
    own_c,
    own_p,
    pair_s,
    pair_r,
    zs,
    zin_c,
    zin_p,
    dqs,
    dqr,
    yslots,
    send,
    recv,
    loc,
):
    f32, bf = jnp.float32, jnp.bfloat16
    s_at = lax.axis_index("seq")
    g = lax.axis_index("grp")
    x, z, c = s_at // (ZN * CN), lax.rem(s_at // CN, ZN), lax.rem(s_at, CN)

    def dev(dx, dz, dc, dg=0):
        xx, zz, gg = lax.rem(x + dx, XN), lax.rem(z + dz, ZN), lax.rem(g + dg, GN)
        cc = 1 - c if dc else c
        return (xx * (ZN * CN) + zz * CN + cc, gg)

    everyone = []
    count = [0]

    def start(src, dst, to):
        cp = pltpu.make_async_remote_copy(
            src_ref=src,
            dst_ref=dst,
            send_sem=send.at[count[0]],
            recv_sem=recv.at[count[0]],
            device_id=to,
            device_id_type=MESH,
        )
        count[0] += 1
        cp.start()
        everyone.append(cp)
        return cp

    def got(*cps):
        for cp in cps:
            cp.wait_recv()

    local_n = [0]

    def local(src, dst):
        cp = pltpu.make_async_copy(src, dst, loc.at[local_n[0]])
        local_n[0] += 1
        cp.start()
        return cp

    def comp_rows(o, other, lo=0, n=TOK):
        u, r = comp_slot(o)
        return keys.at[u, pl.ds(r + other * TOK + lo, n)]

    def prompt_rows(o, other, lo=0, n=PTOK):
        u, r = prompt_slot(o)
        return keys.at[u, pl.ds(r + other * PTOK + lo, n)]

    def code_row(o, other):
        u, r = comp_slot(o)
        return gkc.at[u * 4 + r // TOK + other]

    l_q = local(q_in, gq.at[0])
    l_d = local(d_in, gd.at[0])
    l_kv = local(kv_in, comp_rows(0, 0))
    l_p = local(p_in, slots.at[0])
    code[...] = jnp.broadcast_to(ids[...] * SPAN + pos[...], (8, TOK))
    gqc[0] = code[...]
    u0, r0 = comp_slot(0)
    gkc[u0 * 4 + r0 // TOK] = code[...]

    peer = dev(0, 0, 1)
    barrier = pltpu.get_barrier_semaphore()
    friends = [dev(i, 0, 0) for i in range(1, XN)] + [dev(0, 0, 0, i) for i in range(1, GN)]
    friends += [dev(0, i, 0) for i in range(1, ZN)] + [dev(0, i, 1) for i in range(ZN)]
    for to in friends:
        pl.semaphore_signal(barrier, inc=1, device_id=to, device_id_type=MESH)
    acc[...] = jnp.zeros_like(acc)
    dqt[...] = jnp.zeros_like(dqt)
    for p in range(2):
        st[p, 0:1, :] = jnp.full((1, WIDE), NEG, f32)
        st[p, 1:8, :] = jnp.zeros((7, WIDE), f32)
    for cp in (l_p, l_kv, l_q, l_d):
        cp.wait()
    pl.semaphore_wait(barrier, len(friends))

    y_cps = [start(slots.at[0], slots.at[GN - i], dev(0, 0, 0, i)) for i in range(1, GN)]
    code_cps = [start(code, code_row(0, 1), peer)]
    for i in range(1, ZN):
        code_cps.append(start(code, code_row(ZN - i, 0), dev(0, i, 0)))
        code_cps.append(start(code, code_row(ZN - i, 1), dev(0, i, 1)))
    for i in range(1, XN):
        code_cps.append(start(code, gqc.at[XN - i], dev(i, 0, 0)))
    k_cps, r_cps, p_cps, rp_cps, xq, xd = {}, {}, {}, {}, {}, {}
    mine_k = comp_rows(0, 0)
    xq[3] = start(gq.at[0], gq.at[3], dev(1, 0, 0))
    xd[1] = start(gd.at[0], gd.at[1], dev(3, 0, 0))
    for i in (1, 7):
        k_cps[8 - i] = start(mine_k, comp_rows(8 - i, 0), dev(0, i, 0))
    r_cps[0] = start(mine_k, comp_rows(0, 1), peer)
    for i in (2, 6):
        k_cps[8 - i] = start(mine_k, comp_rows(8 - i, 0), dev(0, i, 0))
    xd[3] = start(gd.at[0], gd.at[3], dev(1, 0, 0))
    xq[1] = start(gq.at[0], gq.at[1], dev(3, 0, 0))

    def relay(*os):
        for o in os:
            r_cps[o] = start(comp_rows(o, 0), comp_rows(o, 1), peer)

    def relay_p(*os):
        for o in os:
            rp_cps[o] = start(prompt_rows(o, 0), prompt_rows(o, 1), peer)

    def loop(n, body):
        def step(j, _):
            body(j)
            return 0

        lax.fori_loop(0, n, step, 0)

    def widen(j):
        wide[j // 4, pl.ds(pl.multiple_of(lax.rem(j, 4) * TOK, TOK), TOK), :] = jnp.broadcast_to(
            gkc[j, 0:1, :], (TOK, TOK)
        ).T

    def spread(i):
        p, at = token_slot(i)
        for h in range(H):
            rows = slice(at + h * TOK, at + (h + 1) * TOK)
            qs[p, rows, :] = gq[i, :, h * DH : (h + 1) * DH]
            ds[p, rows, :] = gd[i, :, h * DH : (h + 1) * DH]

    def visible(u, p):
        masks = []
        for i in PAIRS[p]:
            qc = gqc[i, 0:1, :]
            kc = wide[u]
            base = qc - jnp.bitwise_and(qc, SPAN - 1)
            masks += [(kc <= qc) & (kc >= base)] * H
        return jnp.concatenate(masks, 1)

    def stat_tile(u, p, masked):
        k = keys[u]
        s = nt(k[:, :DH], qs[p])
        if masked:
            s = jnp.where(visible(u, p), s, NEG)
        s = s * C2
        logit[u, p] = s
        dp = nt(k[:, DH:], ds[p])
        m = st[p, 0:1, :]
        m2 = jnp.maximum(m, jnp.max(s, 0, keepdims=True))
        e = jnp.exp2(s - m2)
        a = jnp.exp2(m - m2)
        st[p, 0:1, :] = m2
        st[p, 1:2, :] = st[p, 1:2, :] * a + jnp.sum(e, 0, keepdims=True)
        st[p, 2:3, :] = st[p, 2:3, :] * a + jnp.sum(e * dp, 0, keepdims=True)

    spread(0)
    got(*y_cps)
    total = jnp.zeros((PTOK, 2 * DH), f32)
    for i in range(GN):
        w = (owned[lax.rem(g + i, GN)] == g).astype(f32)
        total = total + slots[i].astype(f32) * w
    mine[...] = total.astype(bf)
    for i in (1, 7, 2, 6):
        p_cps[8 - i] = start(mine, prompt_rows(8 - i, 0), dev(0, i, 0))
    rp_cps[0] = start(mine, prompt_rows(0, 1), peer)
    u, r = prompt_slot(0)
    keys[u, r : r + PTOK, :] = mine[...]
    got(k_cps[1], k_cps[7])
    relay(1, 7)
    got(*code_cps)
    loop(4 * 4, widen)
    half, phalf = TOK // 2, PTOK // 2
    got(k_cps[2], k_cps[6])
    k_cps[5] = start(comp_rows(6, 0), comp_rows(5, 0), dev(0, 1, 0))
    k_cps[3] = start(comp_rows(2, 0), comp_rows(3, 0), dev(0, 7, 0))
    far = [
        start(comp_rows(6, 0, 0, half), comp_rows(4, 0, 0, half), dev(0, 2, 0)),
        start(comp_rows(2, 0, half, half), comp_rows(4, 0, half, half), dev(0, 6, 0)),
    ]
    relay(2, 6)
    got(xq[3])
    xq[2] = start(gq.at[3], gq.at[2], dev(1, 0, 0))
    got(xd[1])
    xd[2] = start(gd.at[1], gd.at[2], dev(3, 0, 0))
    got(p_cps[1], p_cps[7], p_cps[2], p_cps[6])
    p_cps[5] = start(prompt_rows(6, 0), prompt_rows(5, 0), dev(0, 1, 0))
    p_cps[3] = start(prompt_rows(2, 0), prompt_rows(3, 0), dev(0, 7, 0))
    pfar = [
        start(prompt_rows(6, 0, 0, phalf), prompt_rows(4, 0, 0, phalf), dev(0, 2, 0)),
        start(prompt_rows(2, 0, phalf, phalf), prompt_rows(4, 0, phalf, phalf), dev(0, 6, 0)),
    ]
    relay_p(1, 7, 2, 6)
    got(xd[3], xq[1])
    spread(1)
    spread(3)
    got(r_cps[1], r_cps[7], r_cps[2], r_cps[6])
    loop(2, lambda u: stat_tile(u, 0, True))
    got(k_cps[3], k_cps[5], *far)
    relay(3, 5, 4)
    got(rp_cps[0], rp_cps[1], rp_cps[7], rp_cps[2])
    stat_tile(4, 0, False)
    got(p_cps[3], p_cps[5], *pfar)
    relay_p(3, 5, 4)
    got(r_cps[0], r_cps[3], r_cps[5], r_cps[4])
    loop(2, lambda u: stat_tile(2 + u, 0, True))
    got(rp_cps[6], rp_cps[3], rp_cps[5], rp_cps[4])
    stat_tile(5, 0, False)
    st_cps = []

    def share(i):
        p, at = token_slot(i)
        for j in range(1, XN):
            p2, at2 = token_slot((i - j) % XN)
            to = sbuf.at[XN - 1 - j, p2, :, pl.ds(at2, ROWS)]
            st_cps.append(start(st.at[p, :, pl.ds(at, ROWS)], to, dev(j, 0, 0)))

    share(1)
    share(3)
    got(xq[2], xd[2])
    spread(2)
    loop(4, lambda u: stat_tile(u, 1, True))
    loop(2, lambda u: stat_tile(4 + u, 1, False))
    share(0)
    share(2)
    got(*st_cps)
    for i in range(2):
        parts = [st[i]] + [sbuf[j, i] for j in range(XN - 1)]
        m = parts[0][0:1]
        for p in parts[1:]:
            m = jnp.maximum(m, p[0:1])
        l = jnp.zeros_like(m)
        w = jnp.zeros_like(m)
        for p in parts:
            a = jnp.exp2(p[0:1] - m)
            l = l + p[1:2] * a
            w = w + p[2:3] * a
        norm[i, 0:1, :] = m + jnp.log2(l)
        norm[i, 1:2, :] = w / l

    def grad_tile(e, u, i, lo=0, n=UNIT):
        kk = keys[u, lo : lo + n]
        qrow, drow = qs[i], ds[i]
        p = jnp.exp2(logit[u, i, lo : lo + n] - norm[i, 0:1, :])
        dl = (p * (nt(kk[:, DH:], drow) - norm[i, 1:2, :])).astype(bf)
        acc[e, :n, :DH] += nn(dl, qrow)
        acc[e, :n, DH:] += nn(p.astype(bf), drow)
        dqt[i] += tn(kk[:, :DH], dl)

    pair_cps, z_cps = {}, {}

    def emit(e, n, tiles):
        for t in range(tiles):
            r = (t * 2 + 1) * n
            pair_s[e, t * n : (t + 1) * n, :DH] = (acc[e, r : r + n, :DH] * SCALE).astype(bf)
            pair_s[e, t * n : (t + 1) * n, DH:] = acc[e, r : r + n, DH:].astype(bf)
        rows = pl.ds(0, n * tiles)
        pair_cps[e] = start(pair_s.at[e, rows], pair_r.at[e, rows], peer)

    def forward(e, n, offsets, own, zin):
        got(pair_cps[e])
        for t, o in enumerate(offsets):
            rows = slice(t * n, (t + 1) * n)
            both_k = acc[e, t * 2 * n : (t * 2 + 1) * n, :DH] * SCALE + pair_r[e, rows, :DH].astype(f32)
            both_v = acc[e, t * 2 * n : (t * 2 + 1) * n, DH:] + pair_r[e, rows, DH:].astype(f32)
            if o == 0:
                own[:, :DH] = both_k
                own[:, DH:] = both_v
            else:
                zs[e, rows, :DH] = both_k.astype(bf)
                zs[e, rows, DH:] = both_v.astype(bf)
                z_cps[(e, o)] = start(zs.at[e, pl.ds(t * n, n)], zin.at[ZN - 1 - o], dev(0, o, 0))

    dq_cps = []

    def put_query(i):
        p, at = token_slot(i)
        for h in range(H):
            part = dqt[p, :, at + h * TOK : at + (h + 1) * TOK].T * SCALE
            dqs[i, :, h * DH : (h + 1) * DH] = part.astype(bf)
        if i:
            dq_cps.append(start(dqs.at[i], dqr.at[XN - 1 - i], dev(i, 0, 0)))

    loop(2, lambda i: grad_tile(5, 5, i))
    emit(5, PTOK, 4)
    loop(2, lambda i: grad_tile(4, 4, i))
    emit(4, PTOK, 4)
    forward(5, PTOK, PROMPT_AT[4:], own_p, zin_p)
    loop(2, lambda i: grad_tile(3, 3, i, 0, UNIT // 2))
    emit(3, TOK, 1)
    forward(4, PTOK, PROMPT_AT[:4], own_p, zin_p)
    loop(2, lambda i: grad_tile(2, 2, i))
    emit(2, TOK, 2)
    forward(3, TOK, COMP_AT[6:7], own_c, zin_c)
    loop(2, lambda i: grad_tile(1, 1, i))
    emit(1, TOK, 2)
    forward(2, TOK, COMP_AT[4:6], own_c, zin_c)
    grad_tile(0, 0, 1)
    grad_tile(6, 3, 1, UNIT // 2, UNIT // 2)
    put_query(2)
    forward(1, TOK, COMP_AT[2:4], own_c, zin_c)
    put_query(0)
    got(*[cp for (e, o), cp in z_cps.items() if e in (4, 5)])
    total = own_p[...]
    for j in range(ZN - 1):
        total = total + zin_p[j].astype(f32)
    yslots[0] = total.astype(bf)
    my_cps = [start(yslots.at[0], yslots.at[GN - j], dev(0, 0, 0, j)) for j in range(1, GN)]
    grad_tile(0, 0, 0)
    emit(0, TOK, 2)
    grad_tile(6, 3, 0, UNIT // 2, UNIT // 2)
    emit(6, TOK, 1)
    put_query(1)
    put_query(3)
    forward(0, TOK, COMP_AT[0:2], own_c, zin_c)
    forward(6, TOK, COMP_AT[7:], own_c, zin_c)
    got(*my_cps)
    total = jnp.zeros((PTOK, 2 * DH), f32)
    wanted = owned[g]
    for i in range(GN):
        w = (wanted == lax.rem(g + i, GN)).astype(f32)
        total = total + yslots[i].astype(f32) * w
    dp_out[...] = total.astype(bf)
    got(*dq_cps)
    total = dqs[0].astype(f32)
    for j in range(XN - 1):
        total = total + dqr[j].astype(f32)
    dq_out[...] = total.astype(bf)
    got(*[cp for (e, o), cp in z_cps.items() if e not in (4, 5)])
    total = own_c[...]
    for j in range(ZN - 1):
        total = total + zin_c[j].astype(f32)
    dc_out[...] = total.astype(bf)
    for cp in everyone:
        cp.wait_send()


def shards(queries, comp_kv, out_grad, comp_ids, comp_pos, prompt_kv, owned_prompt):
    bf, f32, i32 = jnp.bfloat16, jnp.float32, jnp.int32
    hbm = pl.BlockSpec(memory_space=pl.ANY)
    vmem = pl.BlockSpec(memory_space=pltpu.VMEM)
    smem = pl.BlockSpec(memory_space=pltpu.SMEM)
    grad_q, grad_c, grad_p = pl.pallas_call(
        kernel,
        out_shape=[
            jax.ShapeDtypeStruct((TOK, ROWS), bf),
            jax.ShapeDtypeStruct((TOK, 2 * DH), bf),
            jax.ShapeDtypeStruct((PTOK, 2 * DH), bf),
        ],
        in_specs=[smem, vmem, vmem] + [hbm] * 4,
        out_specs=[vmem] * 3,
        scratch_shapes=[
            pltpu.VMEM((8, TOK), i32),
            pltpu.VMEM((XN, TOK, ROWS), bf),
            pltpu.VMEM((XN, TOK, ROWS), bf),
            pltpu.VMEM((XN, 8, TOK), i32),
            pltpu.VMEM((16, 8, TOK), i32),
            pltpu.VMEM((6, UNIT, 2 * DH), bf),
            pltpu.VMEM((4, UNIT, TOK), i32),
            pltpu.VMEM((2, WIDE, DH), bf),
            pltpu.VMEM((2, WIDE, DH), bf),
            pltpu.VMEM((GN, PTOK, 2 * DH), bf),
            pltpu.VMEM((PTOK, 2 * DH), bf),
            pltpu.VMEM((2, 8, WIDE), f32),
            pltpu.VMEM((XN - 1, 2, 8, WIDE), f32),
            pltpu.VMEM((2, 8, WIDE), f32),
            pltpu.VMEM((6, 2, UNIT, WIDE), f32),
            pltpu.VMEM((7, UNIT, 2 * DH), f32),
            pltpu.VMEM((2, DH, WIDE), f32),
            pltpu.VMEM((TOK, 2 * DH), f32),
            pltpu.VMEM((PTOK, 2 * DH), f32),
            pltpu.VMEM((7, UNIT // 2, 2 * DH), bf),
            pltpu.VMEM((7, UNIT // 2, 2 * DH), bf),
            pltpu.VMEM((7, UNIT // 2, 2 * DH), bf),
            pltpu.VMEM((ZN - 1, TOK, 2 * DH), bf),
            pltpu.VMEM((ZN - 1, PTOK, 2 * DH), bf),
            pltpu.VMEM((XN, TOK, ROWS), bf),
            pltpu.VMEM((XN - 1, TOK, ROWS), bf),
            pltpu.VMEM((GN, PTOK, 2 * DH), bf),
            pltpu.SemaphoreType.DMA((N_SEM,)),
            pltpu.SemaphoreType.DMA((N_SEM,)),
            pltpu.SemaphoreType.DMA((4,)),
        ],
        compiler_params=pltpu.CompilerParams(
            collective_id=0, has_side_effects=True, vmem_limit_bytes=62 * 1024 * 1024
        ),
    )(owned_prompt, comp_ids, comp_pos, queries[0], out_grad[0], comp_kv[0], prompt_kv[0])
    return grad_q[None], grad_c[None], grad_p[None]


def solution(mesh):
    placed = (
        P("grp", "seq", None),
        P("grp", "seq", None),
        P("grp", "seq", None),
        P("grp", "seq"),
        P("grp", "seq"),
        P("grp", "seq", None),
        P(),
    )
    return jax.shard_map(
        shards,
        mesh=mesh,
        in_specs=placed,
        out_specs=(P("grp", "seq", None), P("grp", "seq", None), P("grp", "seq", None)),
        check_vma=False,
    )
```

```python
import math

import jax
import jax.numpy as jnp
from jax import lax
from jax.experimental import pallas as pl
from jax.experimental.pallas import tpu as pltpu
from jax.sharding import PartitionSpec as P

XN = 4
ZN = 8
CN = 2
GN = 4
H = 5
DH = 128
TOK = 128
PTOK = 64
ROWS = H * TOK
UNIT = 512
SPAN = 4096
SCALE = 1.0 / math.sqrt(DH)
C2 = SCALE * 1.4426950408889634
NEG = -1e30
MESH = pl.DeviceIdType.MESH
N_SEM = 112

COMP_AT = [1, 7, 2, 6, 3, 5, 4, 0]
PROMPT_AT = [0, 1, 7, 2, 6, 3, 5, 4]
PAIRS = [(1, 3), (0, 2)]
WIDE = 2 * ROWS


def token_slot(i):
    for p, pair in enumerate(PAIRS):
        if i in pair:
            return p, pair.index(i) * ROWS


def comp_slot(o):
    at = COMP_AT.index(o)
    return at // 2, (at % 2) * CN * TOK


def prompt_slot(o):
    at = PROMPT_AT.index(o)
    return 4 + at // 4, (at % 4) * CN * PTOK


def nt(a, b):
    return lax.dot_general(a, b, (((1,), (1,)), ((), ())), preferred_element_type=jnp.float32)


def nn(a, b):
    return lax.dot_general(a, b, (((1,), (0,)), ((), ())), preferred_element_type=jnp.float32)


def tn(a, b):
    return lax.dot_general(a, b, (((0,), (0,)), ((), ())), preferred_element_type=jnp.float32)


def kernel(
    owned,
    ids,
    pos,
    q_in,
    d_in,
    kv_in,
    p_in,
    dq_out,
    dc_out,
    dp_out,
    code,
    gq,
    gd,
    gqc,
    gkc,
    keys,
    wide,
    qs,
    ds,
    slots,
    mine,
    st,
    sbuf,
    norm,
    logit,
    acc,
    dqt,
    own_c,
    own_p,
    pair_s,
    pair_r,
    zs,
    zin_c,
    zin_p,
    dqs,
    dqr,
    yslots,
    send,
    recv,
    loc,
):
    f32, bf = jnp.float32, jnp.bfloat16
    s_at = lax.axis_index("seq")
    g = lax.axis_index("grp")
    x, z, c = s_at // (ZN * CN), lax.rem(s_at // CN, ZN), lax.rem(s_at, CN)

    def dev(dx, dz, dc, dg=0):
        xx, zz, gg = lax.rem(x + dx, XN), lax.rem(z + dz, ZN), lax.rem(g + dg, GN)
        cc = 1 - c if dc else c
        return (xx * (ZN * CN) + zz * CN + cc, gg)

    everyone = []
    count = [0]

    def start(src, dst, to):
        cp = pltpu.make_async_remote_copy(
            src_ref=src,
            dst_ref=dst,
            send_sem=send.at[count[0]],
            recv_sem=recv.at[count[0]],
            device_id=to,
            device_id_type=MESH,
        )
        count[0] += 1
        cp.start()
        everyone.append(cp)
        return cp

    def got(*cps):
        for cp in cps:
            cp.wait_recv()

    local_n = [0]

    def local(src, dst):
        cp = pltpu.make_async_copy(src, dst, loc.at[local_n[0]])
        local_n[0] += 1
        cp.start()
        return cp

    def comp_rows(o, other, lo=0, n=TOK):
        u, r = comp_slot(o)
        return keys.at[u, pl.ds(r + other * TOK + lo, n)]

    def prompt_rows(o, other, lo=0, n=PTOK):
        u, r = prompt_slot(o)
        return keys.at[u, pl.ds(r + other * PTOK + lo, n)]

    def code_row(o, other):
        u, r = comp_slot(o)
        return gkc.at[u * 4 + r // TOK + other]

    l_q = local(q_in, gq.at[0])
    l_d = local(d_in, gd.at[0])
    l_kv = local(kv_in, comp_rows(0, 0))
    l_p = local(p_in, slots.at[0])
    code[...] = jnp.broadcast_to(ids[...] * SPAN + pos[...], (8, TOK))
    gqc[0] = code[...]
    u0, r0 = comp_slot(0)
    gkc[u0 * 4 + r0 // TOK] = code[...]

    peer = dev(0, 0, 1)
    barrier = pltpu.get_barrier_semaphore()
    friends = [dev(i, 0, 0) for i in range(1, XN)] + [dev(0, 0, 0, i) for i in range(1, GN)]
    friends += [dev(0, i, 0) for i in range(1, ZN)] + [dev(0, i, 1) for i in range(ZN)]
    for to in friends:
        pl.semaphore_signal(barrier, inc=1, device_id=to, device_id_type=MESH)
    acc[...] = jnp.zeros_like(acc)
    dqt[...] = jnp.zeros_like(dqt)
    for p in range(2):
        st[p, 0:1, :] = jnp.full((1, WIDE), NEG, f32)
        st[p, 1:8, :] = jnp.zeros((7, WIDE), f32)
    for cp in (l_p, l_kv, l_q, l_d):
        cp.wait()
    pl.semaphore_wait(barrier, len(friends))

    y_cps = [start(slots.at[0], slots.at[GN - i], dev(0, 0, 0, i)) for i in range(1, GN)]
    code_cps = [start(code, code_row(0, 1), peer)]
    for i in range(1, ZN):
        code_cps.append(start(code, code_row(ZN - i, 0), dev(0, i, 0)))
        code_cps.append(start(code, code_row(ZN - i, 1), dev(0, i, 1)))
    for i in range(1, XN):
        code_cps.append(start(code, gqc.at[XN - i], dev(i, 0, 0)))
    k_cps, r_cps, p_cps, rp_cps, xq, xd = {}, {}, {}, {}, {}, {}
    mine_k = comp_rows(0, 0)
    xq[3] = start(gq.at[0], gq.at[3], dev(1, 0, 0))
    xd[1] = start(gd.at[0], gd.at[1], dev(3, 0, 0))
    for i in (1, 7):
        k_cps[8 - i] = start(mine_k, comp_rows(8 - i, 0), dev(0, i, 0))
    r_cps[0] = start(mine_k, comp_rows(0, 1), peer)
    for i in (2, 6):
        k_cps[8 - i] = start(mine_k, comp_rows(8 - i, 0), dev(0, i, 0))
    xd[3] = start(gd.at[0], gd.at[3], dev(1, 0, 0))
    xq[1] = start(gq.at[0], gq.at[1], dev(3, 0, 0))

    def relay(*os):
        for o in os:
            r_cps[o] = start(comp_rows(o, 0), comp_rows(o, 1), peer)

    def relay_p(*os):
        for o in os:
            rp_cps[o] = start(prompt_rows(o, 0), prompt_rows(o, 1), peer)

    def loop(n, body):
        def step(j, _):
            body(j)
            return 0

        lax.fori_loop(0, n, step, 0)

    def widen(j):
        wide[j // 4, pl.ds(pl.multiple_of(lax.rem(j, 4) * TOK, TOK), TOK), :] = jnp.broadcast_to(
            gkc[j, 0:1, :], (TOK, TOK)
        ).T

    def spread(i):
        p, at = token_slot(i)
        for h in range(H):
            rows = slice(at + h * TOK, at + (h + 1) * TOK)
            qs[p, rows, :] = gq[i, :, h * DH : (h + 1) * DH]
            ds[p, rows, :] = gd[i, :, h * DH : (h + 1) * DH]

    def visible(u, p, half):
        masks = []
        for i in PAIRS[p] if half is None else [PAIRS[p][half]]:
            qc = gqc[i, 0:1, :]
            kc = wide[u]
            base = qc - jnp.bitwise_and(qc, SPAN - 1)
            masks += [(kc <= qc) & (kc >= base)] * H
        return jnp.concatenate(masks, 1)

    def stat_tile(u, p, masked, half=None):
        at = slice(0, WIDE) if half is None else slice(half * ROWS, (half + 1) * ROWS)
        k = keys[u]
        s = nt(k[:, :DH], qs[p, at])
        if masked:
            s = jnp.where(visible(u, p, half), s, NEG)
        s = s * C2
        logit[u, p, :, at] = s
        dp = nt(k[:, DH:], ds[p, at])
        m = st[p, 0:1, at]
        m2 = jnp.maximum(m, jnp.max(s, 0, keepdims=True))
        e = jnp.exp2(s - m2)
        a = jnp.exp2(m - m2)
        st[p, 0:1, at] = m2
        st[p, 1:2, at] = st[p, 1:2, at] * a + jnp.sum(e, 0, keepdims=True)
        st[p, 2:3, at] = st[p, 2:3, at] * a + jnp.sum(e * dp, 0, keepdims=True)

    spread(0)
    got(*y_cps)
    total = jnp.zeros((PTOK, 2 * DH), f32)
    for i in range(GN):
        w = (owned[lax.rem(g + i, GN)] == g).astype(f32)
        total = total + slots[i].astype(f32) * w
    mine[...] = total.astype(bf)
    for i in (1, 7, 2, 6):
        p_cps[8 - i] = start(mine, prompt_rows(8 - i, 0), dev(0, i, 0))
    rp_cps[0] = start(mine, prompt_rows(0, 1), peer)
    u, r = prompt_slot(0)
    keys[u, r : r + PTOK, :] = mine[...]
    got(k_cps[1], k_cps[7])
    relay(1, 7)
    got(*code_cps)
    loop(4 * 4, widen)
    half, phalf = TOK // 2, PTOK // 2
    got(k_cps[2], k_cps[6])
    k_cps[5] = start(comp_rows(6, 0), comp_rows(5, 0), dev(0, 1, 0))
    k_cps[3] = start(comp_rows(2, 0), comp_rows(3, 0), dev(0, 7, 0))
    far = [
        start(comp_rows(6, 0, 0, half), comp_rows(4, 0, 0, half), dev(0, 2, 0)),
        start(comp_rows(2, 0, half, half), comp_rows(4, 0, half, half), dev(0, 6, 0)),
    ]
    relay(2, 6)
    got(xq[3])
    xq[2] = start(gq.at[3], gq.at[2], dev(1, 0, 0))
    got(xd[1])
    xd[2] = start(gd.at[1], gd.at[2], dev(3, 0, 0))
    got(r_cps[1], r_cps[7])
    stat_tile(0, 1, True, 0)
    got(r_cps[2], r_cps[6])
    stat_tile(1, 1, True, 0)
    got(xd[3], xq[1])
    spread(1)
    spread(3)
    stat_tile(0, 0, True)
    got(p_cps[1], p_cps[7], p_cps[2], p_cps[6])
    p_cps[5] = start(prompt_rows(6, 0), prompt_rows(5, 0), dev(0, 1, 0))
    p_cps[3] = start(prompt_rows(2, 0), prompt_rows(3, 0), dev(0, 7, 0))
    pfar = [
        start(prompt_rows(6, 0, 0, phalf), prompt_rows(4, 0, 0, phalf), dev(0, 2, 0)),
        start(prompt_rows(2, 0, phalf, phalf), prompt_rows(4, 0, phalf, phalf), dev(0, 6, 0)),
    ]
    relay_p(1, 7, 2, 6)
    got(k_cps[3], k_cps[5], *far)
    relay(3, 5, 4)
    stat_tile(1, 0, True)
    got(r_cps[0], r_cps[3], r_cps[5], r_cps[4])
    loop(2, lambda u: stat_tile(2 + u, 0, True))
    got(xq[2], xd[2])
    spread(2)
    got(p_cps[3], p_cps[5], *pfar)
    relay_p(3, 5, 4)
    loop(2, lambda u: stat_tile(2 + u, 1, True))
    got(rp_cps[0], rp_cps[1], rp_cps[7], rp_cps[2])
    got(rp_cps[6], rp_cps[3], rp_cps[5], rp_cps[4])
    loop(2, lambda u: stat_tile(4 + u, 0, False))
    st_cps = []

    def share(i):
        p, at = token_slot(i)
        for j in range(1, XN):
            p2, at2 = token_slot((i - j) % XN)
            to = sbuf.at[XN - 1 - j, p2, :, pl.ds(at2, ROWS)]
            st_cps.append(start(st.at[p, :, pl.ds(at, ROWS)], to, dev(j, 0, 0)))

    share(1)
    share(3)
    loop(2, lambda u: stat_tile(u, 1, True, 1))
    loop(2, lambda u: stat_tile(4 + u, 1, False))
    share(0)
    share(2)
    got(*st_cps)
    for i in range(2):
        parts = [st[i]] + [sbuf[j, i] for j in range(XN - 1)]
        m = parts[0][0:1]
        for p in parts[1:]:
            m = jnp.maximum(m, p[0:1])
        l = jnp.zeros_like(m)
        w = jnp.zeros_like(m)
        for p in parts:
            a = jnp.exp2(p[0:1] - m)
            l = l + p[1:2] * a
            w = w + p[2:3] * a
        norm[i, 0:1, :] = m + jnp.log2(l)
        norm[i, 1:2, :] = w / l

    def grad_tile(e, u, i, lo=0, n=UNIT):
        kk = keys[u, lo : lo + n]
        qrow, drow = qs[i], ds[i]
        p = jnp.exp2(logit[u, i, lo : lo + n] - norm[i, 0:1, :])
        dl = (p * (nt(kk[:, DH:], drow) - norm[i, 1:2, :])).astype(bf)
        acc[e, :n, :DH] += nn(dl, qrow)
        acc[e, :n, DH:] += nn(p.astype(bf), drow)
        dqt[i] += tn(kk[:, :DH], dl)

    pair_cps, z_cps = {}, {}

    def emit(e, n, tiles):
        for t in range(tiles):
            r = (t * 2 + 1) * n
            pair_s[e, t * n : (t + 1) * n, :DH] = (acc[e, r : r + n, :DH] * SCALE).astype(bf)
            pair_s[e, t * n : (t + 1) * n, DH:] = acc[e, r : r + n, DH:].astype(bf)
        rows = pl.ds(0, n * tiles)
        pair_cps[e] = start(pair_s.at[e, rows], pair_r.at[e, rows], peer)

    def forward(e, n, offsets, own, zin):
        got(pair_cps[e])
        for t, o in enumerate(offsets):
            rows = slice(t * n, (t + 1) * n)
            both_k = acc[e, t * 2 * n : (t * 2 + 1) * n, :DH] * SCALE + pair_r[e, rows, :DH].astype(f32)
            both_v = acc[e, t * 2 * n : (t * 2 + 1) * n, DH:] + pair_r[e, rows, DH:].astype(f32)
            if o == 0:
                own[:, :DH] = both_k
                own[:, DH:] = both_v
            else:
                zs[e, rows, :DH] = both_k.astype(bf)
                zs[e, rows, DH:] = both_v.astype(bf)
                z_cps[(e, o)] = start(zs.at[e, pl.ds(t * n, n)], zin.at[ZN - 1 - o], dev(0, o, 0))

    dq_cps = []

    def put_query(i):
        p, at = token_slot(i)
        for h in range(H):
            part = dqt[p, :, at + h * TOK : at + (h + 1) * TOK].T * SCALE
            dqs[i, :, h * DH : (h + 1) * DH] = part.astype(bf)
        if i:
            dq_cps.append(start(dqs.at[i], dqr.at[XN - 1 - i], dev(i, 0, 0)))

    loop(2, lambda i: grad_tile(5, 5, i))
    emit(5, PTOK, 4)
    loop(2, lambda i: grad_tile(4, 4, i))
    emit(4, PTOK, 4)
    forward(5, PTOK, PROMPT_AT[4:], own_p, zin_p)
    loop(2, lambda i: grad_tile(3, 3, i, 0, UNIT // 2))
    emit(3, TOK, 1)
    forward(4, PTOK, PROMPT_AT[:4], own_p, zin_p)
    loop(2, lambda i: grad_tile(2, 2, i))
    emit(2, TOK, 2)
    forward(3, TOK, COMP_AT[6:7], own_c, zin_c)
    loop(2, lambda i: grad_tile(1, 1, i))
    emit(1, TOK, 2)
    forward(2, TOK, COMP_AT[4:6], own_c, zin_c)
    grad_tile(0, 0, 1)
    grad_tile(6, 3, 1, UNIT // 2, UNIT // 2)
    put_query(2)
    forward(1, TOK, COMP_AT[2:4], own_c, zin_c)
    put_query(0)
    got(*[cp for (e, o), cp in z_cps.items() if e in (4, 5)])
    total = own_p[...]
    for j in range(ZN - 1):
        total = total + zin_p[j].astype(f32)
    yslots[0] = total.astype(bf)
    my_cps = [start(yslots.at[0], yslots.at[GN - j], dev(0, 0, 0, j)) for j in range(1, GN)]
    grad_tile(0, 0, 0)
    emit(0, TOK, 2)
    grad_tile(6, 3, 0, UNIT // 2, UNIT // 2)
    emit(6, TOK, 1)
    put_query(1)
    put_query(3)
    forward(0, TOK, COMP_AT[0:2], own_c, zin_c)
    forward(6, TOK, COMP_AT[7:], own_c, zin_c)
    got(*my_cps)
    total = jnp.zeros((PTOK, 2 * DH), f32)
    wanted = owned[g]
    for i in range(GN):
        w = (wanted == lax.rem(g + i, GN)).astype(f32)
        total = total + yslots[i].astype(f32) * w
    dp_out[...] = total
    got(*dq_cps)
    total = dqs[0].astype(f32)
    for j in range(XN - 1):
        total = total + dqr[j].astype(f32)
    dq_out[...] = total
    got(*[cp for (e, o), cp in z_cps.items() if e not in (4, 5)])
    total = own_c[...]
    for j in range(ZN - 1):
        total = total + zin_c[j].astype(f32)
    dc_out[...] = total
    for cp in everyone:
        cp.wait_send()


def shards(queries, comp_kv, out_grad, comp_ids, comp_pos, prompt_kv, owned_prompt):
    bf, f32, i32 = jnp.bfloat16, jnp.float32, jnp.int32
    hbm = pl.BlockSpec(memory_space=pl.ANY)
    vmem = pl.BlockSpec(memory_space=pltpu.VMEM)
    smem = pl.BlockSpec(memory_space=pltpu.SMEM)
    grad_q, grad_c, grad_p = pl.pallas_call(
        kernel,
        out_shape=[
            jax.ShapeDtypeStruct((TOK, ROWS), f32),
            jax.ShapeDtypeStruct((TOK, 2 * DH), f32),
            jax.ShapeDtypeStruct((PTOK, 2 * DH), f32),
        ],
        in_specs=[smem, vmem, vmem] + [hbm] * 4,
        out_specs=[vmem] * 3,
        scratch_shapes=[
            pltpu.VMEM((8, TOK), i32),
            pltpu.VMEM((XN, TOK, ROWS), bf),
            pltpu.VMEM((XN, TOK, ROWS), bf),
            pltpu.VMEM((XN, 8, TOK), i32),
            pltpu.VMEM((16, 8, TOK), i32),
            pltpu.VMEM((6, UNIT, 2 * DH), bf),
            pltpu.VMEM((4, UNIT, TOK), i32),
            pltpu.VMEM((2, WIDE, DH), bf),
            pltpu.VMEM((2, WIDE, DH), bf),
            pltpu.VMEM((GN, PTOK, 2 * DH), bf),
            pltpu.VMEM((PTOK, 2 * DH), bf),
            pltpu.VMEM((2, 8, WIDE), f32),
            pltpu.VMEM((XN - 1, 2, 8, WIDE), f32),
            pltpu.VMEM((2, 8, WIDE), f32),
            pltpu.VMEM((6, 2, UNIT, WIDE), f32),
            pltpu.VMEM((7, UNIT, 2 * DH), f32),
            pltpu.VMEM((2, DH, WIDE), f32),
            pltpu.VMEM((TOK, 2 * DH), f32),
            pltpu.VMEM((PTOK, 2 * DH), f32),
            pltpu.VMEM((7, UNIT // 2, 2 * DH), bf),
            pltpu.VMEM((7, UNIT // 2, 2 * DH), bf),
            pltpu.VMEM((7, UNIT // 2, 2 * DH), bf),
            pltpu.VMEM((ZN - 1, TOK, 2 * DH), bf),
            pltpu.VMEM((ZN - 1, PTOK, 2 * DH), bf),
            pltpu.VMEM((XN, TOK, ROWS), bf),
            pltpu.VMEM((XN - 1, TOK, ROWS), bf),
            pltpu.VMEM((GN, PTOK, 2 * DH), bf),
            pltpu.SemaphoreType.DMA((N_SEM,)),
            pltpu.SemaphoreType.DMA((N_SEM,)),
            pltpu.SemaphoreType.DMA((4,)),
        ],
        compiler_params=pltpu.CompilerParams(
            collective_id=0, has_side_effects=True, vmem_limit_bytes=62 * 1024 * 1024
        ),
    )(owned_prompt, comp_ids, comp_pos, queries[0], out_grad[0], comp_kv[0], prompt_kv[0])
    return grad_q[None].astype(bf), grad_c[None].astype(bf), grad_p[None].astype(bf)


def solution(mesh):
    placed = (
        P("grp", "seq", None),
        P("grp", "seq", None),
        P("grp", "seq", None),
        P("grp", "seq"),
        P("grp", "seq"),
        P("grp", "seq", None),
        P(),
    )
    return jax.shard_map(
        shards,
        mesh=mesh,
        in_specs=placed,
        out_specs=(P("grp", "seq", None), P("grp", "seq", None), P("grp", "seq", None)),
        check_vma=False,
    )
```

```python
import math

import jax
import jax.numpy as jnp
from jax import lax
from jax.experimental import pallas as pl
from jax.experimental.pallas import tpu as pltpu
from jax.sharding import PartitionSpec as P

XN = 4
ZN = 8
CN = 2
GN = 4
H = 5
DH = 128
TOK = 128
PTOK = 64
ROWS = H * TOK
UNIT = 512
SPAN = 4096
SCALE = 1.0 / math.sqrt(DH)
C2 = SCALE * 1.4426950408889634
NEG = -1e30
MESH = pl.DeviceIdType.MESH
N_SEM = 112

COMP_AT = [1, 7, 2, 6, 3, 5, 4, 0]
PROMPT_AT = [0, 1, 7, 2, 6, 3, 5, 4]
PAIRS = [(1, 3), (0, 2)]
WIDE = 2 * ROWS


def token_slot(i):
    for p, pair in enumerate(PAIRS):
        if i in pair:
            return p, pair.index(i) * ROWS


def comp_slot(o):
    at = COMP_AT.index(o)
    return at // 2, (at % 2) * CN * TOK


def prompt_slot(o):
    at = PROMPT_AT.index(o)
    return 4 + at // 4, (at % 4) * CN * PTOK


def nt(a, b):
    return lax.dot_general(a, b, (((1,), (1,)), ((), ())), preferred_element_type=jnp.float32)


def nn(a, b):
    return lax.dot_general(a, b, (((1,), (0,)), ((), ())), preferred_element_type=jnp.float32)


def tn(a, b):
    return lax.dot_general(a, b, (((0,), (0,)), ((), ())), preferred_element_type=jnp.float32)


def kernel(
    owned,
    ids,
    pos,
    q_in,
    d_in,
    kv_in,
    p_in,
    dq_out,
    dc_out,
    dp_out,
    code,
    gq,
    gd,
    gqc,
    gkc,
    keys,
    wide,
    qs,
    ds,
    slots,
    mine,
    st,
    sbuf,
    norm,
    logit,
    second,
    acc,
    dqt,
    own_c,
    own_p,
    pair_s,
    pair_r,
    zs,
    zin_c,
    zin_p,
    dqs,
    dqr,
    yslots,
    send,
    recv,
    loc,
):
    f32, bf = jnp.float32, jnp.bfloat16
    s_at = lax.axis_index("seq")
    g = lax.axis_index("grp")
    x, z, c = s_at // (ZN * CN), lax.rem(s_at // CN, ZN), lax.rem(s_at, CN)

    def dev(dx, dz, dc, dg=0):
        xx, zz, gg = lax.rem(x + dx, XN), lax.rem(z + dz, ZN), lax.rem(g + dg, GN)
        cc = 1 - c if dc else c
        return (xx * (ZN * CN) + zz * CN + cc, gg)

    everyone = []
    count = [0]

    def start(src, dst, to):
        cp = pltpu.make_async_remote_copy(
            src_ref=src,
            dst_ref=dst,
            send_sem=send.at[count[0]],
            recv_sem=recv.at[count[0]],
            device_id=to,
            device_id_type=MESH,
        )
        count[0] += 1
        cp.start()
        everyone.append(cp)
        return cp

    def got(*cps):
        for cp in cps:
            cp.wait_recv()

    local_n = [0]

    def local(src, dst):
        cp = pltpu.make_async_copy(src, dst, loc.at[local_n[0]])
        local_n[0] += 1
        cp.start()
        return cp

    def comp_rows(o, other, lo=0, n=TOK):
        u, r = comp_slot(o)
        return keys.at[u, pl.ds(r + other * TOK + lo, n)]

    def prompt_rows(o, other, lo=0, n=PTOK):
        u, r = prompt_slot(o)
        return keys.at[u, pl.ds(r + other * PTOK + lo, n)]

    def code_row(o, other):
        u, r = comp_slot(o)
        return gkc.at[u * 4 + r // TOK + other]

    l_q = local(q_in, gq.at[0])
    l_d = local(d_in, gd.at[0])
    l_kv = local(kv_in, comp_rows(0, 0))
    l_p = local(p_in, slots.at[0])
    code[...] = jnp.broadcast_to(ids[...] * SPAN + pos[...], (8, TOK))
    gqc[0] = code[...]
    u0, r0 = comp_slot(0)
    gkc[u0 * 4 + r0 // TOK] = code[...]

    peer = dev(0, 0, 1)
    barrier = pltpu.get_barrier_semaphore()
    friends = [dev(i, 0, 0) for i in range(1, XN)] + [dev(0, 0, 0, i) for i in range(1, GN)]
    friends += [dev(0, i, 0) for i in range(1, ZN)] + [dev(0, i, 1) for i in range(ZN)]
    for to in friends:
        pl.semaphore_signal(barrier, inc=1, device_id=to, device_id_type=MESH)
    acc[...] = jnp.zeros_like(acc)
    dqt[...] = jnp.zeros_like(dqt)
    for p in range(2):
        st[p, 0:1, :] = jnp.full((1, WIDE), NEG, f32)
        st[p, 1:8, :] = jnp.zeros((7, WIDE), f32)
    for cp in (l_p, l_kv, l_q, l_d):
        cp.wait()
    pl.semaphore_wait(barrier, len(friends))

    y_cps = [start(slots.at[0], slots.at[GN - i], dev(0, 0, 0, i)) for i in range(1, GN)]
    code_cps = [start(code, code_row(0, 1), peer)]
    for i in range(1, ZN):
        code_cps.append(start(code, code_row(ZN - i, 0), dev(0, i, 0)))
        code_cps.append(start(code, code_row(ZN - i, 1), dev(0, i, 1)))
    for i in range(1, XN):
        code_cps.append(start(code, gqc.at[XN - i], dev(i, 0, 0)))
    k_cps, r_cps, p_cps, rp_cps, xq, xd = {}, {}, {}, {}, {}, {}
    mine_k = comp_rows(0, 0)
    xq[3] = start(gq.at[0], gq.at[3], dev(1, 0, 0))
    xd[1] = start(gd.at[0], gd.at[1], dev(3, 0, 0))
    for i in (1, 7):
        k_cps[8 - i] = start(mine_k, comp_rows(8 - i, 0), dev(0, i, 0))
    r_cps[0] = start(mine_k, comp_rows(0, 1), peer)
    for i in (2, 6):
        k_cps[8 - i] = start(mine_k, comp_rows(8 - i, 0), dev(0, i, 0))
    xd[3] = start(gd.at[0], gd.at[3], dev(1, 0, 0))
    xq[1] = start(gq.at[0], gq.at[1], dev(3, 0, 0))

    def relay(*os):
        for o in os:
            r_cps[o] = start(comp_rows(o, 0), comp_rows(o, 1), peer)

    def relay_p(*os):
        for o in os:
            rp_cps[o] = start(prompt_rows(o, 0), prompt_rows(o, 1), peer)

    def loop(n, body):
        def step(j, _):
            body(j)
            return 0

        lax.fori_loop(0, n, step, 0)

    def widen(j):
        wide[j // 4, pl.ds(pl.multiple_of(lax.rem(j, 4) * TOK, TOK), TOK), :] = jnp.broadcast_to(
            gkc[j, 0:1, :], (TOK, TOK)
        ).T

    def spread(i):
        p, at = token_slot(i)
        for h in range(H):
            rows = slice(at + h * TOK, at + (h + 1) * TOK)
            qs[p, rows, :] = gq[i, :, h * DH : (h + 1) * DH]
            ds[p, rows, :] = gd[i, :, h * DH : (h + 1) * DH]

    def visible(u, p, half):
        masks = []
        for i in PAIRS[p] if half is None else [PAIRS[p][half]]:
            qc = gqc[i, 0:1, :]
            kc = wide[u]
            base = qc - jnp.bitwise_and(qc, SPAN - 1)
            masks += [(kc <= qc) & (kc >= base)] * H
        return jnp.concatenate(masks, 1)

    def stat_tile(u, p, masked, half=None):
        at = slice(0, WIDE) if half is None else slice(half * ROWS, (half + 1) * ROWS)
        k = keys[u]
        s = nt(k[:, :DH], qs[p, at])
        if masked:
            s = jnp.where(visible(u, p, half), s, NEG)
        s = s * C2
        logit[u, p, :, at] = s
        dp = nt(k[:, DH:], ds[p, at])
        if not masked:
            second[u - 4, p] = dp
        m = st[p, 0:1, at]
        m2 = jnp.maximum(m, jnp.max(s, 0, keepdims=True))
        e = jnp.exp2(s - m2)
        a = jnp.exp2(m - m2)
        st[p, 0:1, at] = m2
        st[p, 1:2, at] = st[p, 1:2, at] * a + jnp.sum(e, 0, keepdims=True)
        st[p, 2:3, at] = st[p, 2:3, at] * a + jnp.sum(e * dp, 0, keepdims=True)

    spread(0)
    got(*y_cps)
    total = jnp.zeros((PTOK, 2 * DH), f32)
    for i in range(GN):
        w = (owned[lax.rem(g + i, GN)] == g).astype(f32)
        total = total + slots[i].astype(f32) * w
    mine[...] = total.astype(bf)
    for i in (1, 7, 2, 6):
        p_cps[8 - i] = start(mine, prompt_rows(8 - i, 0), dev(0, i, 0))
    rp_cps[0] = start(mine, prompt_rows(0, 1), peer)
    u, r = prompt_slot(0)
    keys[u, r : r + PTOK, :] = mine[...]
    got(k_cps[1], k_cps[7])
    relay(1, 7)
    got(*code_cps)
    loop(4 * 4, widen)
    half, phalf = TOK // 2, PTOK // 2
    got(k_cps[2], k_cps[6])
    k_cps[5] = start(comp_rows(6, 0), comp_rows(5, 0), dev(0, 1, 0))
    k_cps[3] = start(comp_rows(2, 0), comp_rows(3, 0), dev(0, 7, 0))
    far = [
        start(comp_rows(6, 0, 0, half), comp_rows(4, 0, 0, half), dev(0, 2, 0)),
        start(comp_rows(2, 0, half, half), comp_rows(4, 0, half, half), dev(0, 6, 0)),
    ]
    relay(2, 6)
    got(xq[3])
    xq[2] = start(gq.at[3], gq.at[2], dev(1, 0, 0))
    got(xd[1])
    xd[2] = start(gd.at[1], gd.at[2], dev(3, 0, 0))
    got(r_cps[1], r_cps[7])
    stat_tile(0, 1, True, 0)
    got(r_cps[2], r_cps[6])
    stat_tile(1, 1, True, 0)
    got(xd[3], xq[1])
    spread(1)
    spread(3)
    stat_tile(0, 0, True)
    got(p_cps[1], p_cps[7], p_cps[2], p_cps[6])
    p_cps[5] = start(prompt_rows(6, 0), prompt_rows(5, 0), dev(0, 1, 0))
    p_cps[3] = start(prompt_rows(2, 0), prompt_rows(3, 0), dev(0, 7, 0))
    pfar = [
        start(prompt_rows(6, 0, 0, phalf), prompt_rows(4, 0, 0, phalf), dev(0, 2, 0)),
        start(prompt_rows(2, 0, phalf, phalf), prompt_rows(4, 0, phalf, phalf), dev(0, 6, 0)),
    ]
    relay_p(1, 7, 2, 6)
    got(k_cps[3], k_cps[5], *far)
    relay(3, 5, 4)
    stat_tile(1, 0, True)
    got(r_cps[0], r_cps[3], r_cps[5], r_cps[4])
    loop(2, lambda u: stat_tile(2 + u, 0, True))
    got(xq[2], xd[2])
    spread(2)
    loop(2, lambda u: stat_tile(u, 1, True, 1))
    loop(2, lambda u: stat_tile(2 + u, 1, True))
    got(p_cps[3], p_cps[5], *pfar)
    relay_p(3, 5, 4)
    got(rp_cps[0], rp_cps[1], rp_cps[7], rp_cps[2])
    loop(2, lambda p: stat_tile(4, p, False))
    got(rp_cps[6], rp_cps[3], rp_cps[5], rp_cps[4])
    loop(2, lambda p: stat_tile(5, p, False))
    st_cps = []

    def share(i):
        p, at = token_slot(i)
        for j in range(1, XN):
            p2, at2 = token_slot((i - j) % XN)
            to = sbuf.at[XN - 1 - j, p2, :, pl.ds(at2, ROWS)]
            st_cps.append(start(st.at[p, :, pl.ds(at, ROWS)], to, dev(j, 0, 0)))

    for i in range(XN):
        share(i)
    got(*st_cps)
    for i in range(2):
        parts = [st[i]] + [sbuf[j, i] for j in range(XN - 1)]
        m = parts[0][0:1]
        for p in parts[1:]:
            m = jnp.maximum(m, p[0:1])
        l = jnp.zeros_like(m)
        w = jnp.zeros_like(m)
        for p in parts:
            a = jnp.exp2(p[0:1] - m)
            l = l + p[1:2] * a
            w = w + p[2:3] * a
        norm[i, 0:1, :] = m + jnp.log2(l)
        norm[i, 1:2, :] = w / l

    def grad_tile(e, u, i, lo=0, n=UNIT):
        kk = keys[u, lo : lo + n]
        qrow, drow = qs[i], ds[i]
        p = jnp.exp2(logit[u, i, lo : lo + n] - norm[i, 0:1, :])
        dp = second[u - 4, i] if u >= 4 else nt(kk[:, DH:], drow)
        dl = (p * (dp - norm[i, 1:2, :])).astype(bf)
        acc[e, :n, :DH] += nn(dl, qrow)
        acc[e, :n, DH:] += nn(p.astype(bf), drow)
        dqt[i] += tn(kk[:, :DH], dl)

    pair_cps, z_cps = {}, {}

    def emit(e, n, tiles):
        for t in range(tiles):
            r = (t * 2 + 1) * n
            pair_s[e, t * n : (t + 1) * n, :DH] = (acc[e, r : r + n, :DH] * SCALE).astype(bf)
            pair_s[e, t * n : (t + 1) * n, DH:] = acc[e, r : r + n, DH:].astype(bf)
        rows = pl.ds(0, n * tiles)
        pair_cps[e] = start(pair_s.at[e, rows], pair_r.at[e, rows], peer)

    def forward(e, n, offsets, own, zin):
        got(pair_cps[e])
        for t, o in enumerate(offsets):
            rows = slice(t * n, (t + 1) * n)
            both_k = acc[e, t * 2 * n : (t * 2 + 1) * n, :DH] * SCALE + pair_r[e, rows, :DH].astype(f32)
            both_v = acc[e, t * 2 * n : (t * 2 + 1) * n, DH:] + pair_r[e, rows, DH:].astype(f32)
            if o == 0:
                own[:, :DH] = both_k
                own[:, DH:] = both_v
            else:
                zs[e, rows, :DH] = both_k.astype(bf)
                zs[e, rows, DH:] = both_v.astype(bf)
                z_cps[(e, o)] = start(zs.at[e, pl.ds(t * n, n)], zin.at[ZN - 1 - o], dev(0, o, 0))

    dq_cps = []

    def put_query(i):
        p, at = token_slot(i)
        for h in range(H):
            part = dqt[p, :, at + h * TOK : at + (h + 1) * TOK].T * SCALE
            dqs[i, :, h * DH : (h + 1) * DH] = part.astype(bf)
        if i:
            dq_cps.append(start(dqs.at[i], dqr.at[XN - 1 - i], dev(i, 0, 0)))

    loop(2, lambda i: grad_tile(5, 5, i))
    emit(5, PTOK, 4)
    loop(2, lambda i: grad_tile(4, 4, i))
    emit(4, PTOK, 4)
    forward(5, PTOK, PROMPT_AT[4:], own_p, zin_p)
    loop(2, lambda i: grad_tile(3, 3, i, 0, UNIT // 2))
    emit(3, TOK, 1)
    forward(4, PTOK, PROMPT_AT[:4], own_p, zin_p)
    loop(2, lambda i: grad_tile(2, 2, i))
    emit(2, TOK, 2)
    forward(3, TOK, COMP_AT[6:7], own_c, zin_c)
    loop(2, lambda i: grad_tile(1, 1, i))
    emit(1, TOK, 2)
    forward(2, TOK, COMP_AT[4:6], own_c, zin_c)
    grad_tile(0, 0, 1)
    grad_tile(6, 3, 1, UNIT // 2, UNIT // 2)
    put_query(2)
    forward(1, TOK, COMP_AT[2:4], own_c, zin_c)
    put_query(0)
    got(*[cp for (e, o), cp in z_cps.items() if e in (4, 5)])
    total = own_p[...]
    for j in range(ZN - 1):
        total = total + zin_p[j].astype(f32)
    yslots[0] = total.astype(bf)
    my_cps = [start(yslots.at[0], yslots.at[GN - j], dev(0, 0, 0, j)) for j in range(1, GN)]
    grad_tile(0, 0, 0)
    emit(0, TOK, 2)
    grad_tile(6, 3, 0, UNIT // 2, UNIT // 2)
    emit(6, TOK, 1)
    put_query(1)
    put_query(3)
    forward(0, TOK, COMP_AT[0:2], own_c, zin_c)
    forward(6, TOK, COMP_AT[7:], own_c, zin_c)
    got(*my_cps)
    total = jnp.zeros((PTOK, 2 * DH), f32)
    wanted = owned[g]
    for i in range(GN):
        w = (wanted == lax.rem(g + i, GN)).astype(f32)
        total = total + yslots[i].astype(f32) * w
    dp_out[...] = total.astype(bf)
    got(*dq_cps)
    total = dqs[0].astype(f32)
    for j in range(XN - 1):
        total = total + dqr[j].astype(f32)
    dq_out[...] = total.astype(bf)
    got(*[cp for (e, o), cp in z_cps.items() if e not in (4, 5)])
    total = own_c[...]
    for j in range(ZN - 1):
        total = total + zin_c[j].astype(f32)
    dc_out[...] = total.astype(bf)
    for cp in everyone:
        cp.wait_send()


def hand_over(*refs):
    sems = refs[6]
    cps = [pltpu.make_async_copy(refs[i], refs[3 + i], sems.at[i]) for i in range(3)]
    for cp in cps:
        cp.start()
    for cp in cps:
        cp.wait()


def shards(queries, comp_kv, out_grad, comp_ids, comp_pos, prompt_kv, owned_prompt):
    bf, f32, i32 = jnp.bfloat16, jnp.float32, jnp.int32
    hbm = pl.BlockSpec(memory_space=pl.ANY)
    vmem = pl.BlockSpec(memory_space=pltpu.VMEM)
    smem = pl.BlockSpec(memory_space=pltpu.SMEM)
    grad_q, grad_c, grad_p = pl.pallas_call(
        kernel,
        out_shape=[
            jax.ShapeDtypeStruct((TOK, ROWS), bf),
            jax.ShapeDtypeStruct((TOK, 2 * DH), bf),
            jax.ShapeDtypeStruct((PTOK, 2 * DH), bf),
        ],
        in_specs=[smem, vmem, vmem] + [hbm] * 4,
        out_specs=[vmem] * 3,
        scratch_shapes=[
            pltpu.VMEM((8, TOK), i32),
            pltpu.VMEM((XN, TOK, ROWS), bf),
            pltpu.VMEM((XN, TOK, ROWS), bf),
            pltpu.VMEM((XN, 8, TOK), i32),
            pltpu.VMEM((16, 8, TOK), i32),
            pltpu.VMEM((6, UNIT, 2 * DH), bf),
            pltpu.VMEM((4, UNIT, TOK), i32),
            pltpu.VMEM((2, WIDE, DH), bf),
            pltpu.VMEM((2, WIDE, DH), bf),
            pltpu.VMEM((GN, PTOK, 2 * DH), bf),
            pltpu.VMEM((PTOK, 2 * DH), bf),
            pltpu.VMEM((2, 8, WIDE), f32),
            pltpu.VMEM((XN - 1, 2, 8, WIDE), f32),
            pltpu.VMEM((2, 8, WIDE), f32),
            pltpu.VMEM((6, 2, UNIT, WIDE), f32),
            pltpu.VMEM((2, 2, UNIT, WIDE), f32),
            pltpu.VMEM((7, UNIT, 2 * DH), f32),
            pltpu.VMEM((2, DH, WIDE), f32),
            pltpu.VMEM((TOK, 2 * DH), f32),
            pltpu.VMEM((PTOK, 2 * DH), f32),
            pltpu.VMEM((7, UNIT // 2, 2 * DH), bf),
            pltpu.VMEM((7, UNIT // 2, 2 * DH), bf),
            pltpu.VMEM((7, UNIT // 2, 2 * DH), bf),
            pltpu.VMEM((ZN - 1, TOK, 2 * DH), bf),
            pltpu.VMEM((ZN - 1, PTOK, 2 * DH), bf),
            pltpu.VMEM((XN, TOK, ROWS), bf),
            pltpu.VMEM((XN - 1, TOK, ROWS), bf),
            pltpu.VMEM((GN, PTOK, 2 * DH), bf),
            pltpu.SemaphoreType.DMA((N_SEM,)),
            pltpu.SemaphoreType.DMA((N_SEM,)),
            pltpu.SemaphoreType.DMA((4,)),
        ],
        compiler_params=pltpu.CompilerParams(
            collective_id=0, has_side_effects=True, vmem_limit_bytes=64 * 1024 * 1024
        ),
    )(owned_prompt, comp_ids, comp_pos, queries[0], out_grad[0], comp_kv[0], prompt_kv[0])
    results = [grad_q[None], grad_c[None], grad_p[None]]
    return pl.pallas_call(
        hand_over,
        out_shape=[jax.ShapeDtypeStruct(r.shape, r.dtype) for r in results],
        in_specs=[hbm] * 3,
        out_specs=[hbm] * 3,
        scratch_shapes=[pltpu.SemaphoreType.DMA((3,))],
        compiler_params=pltpu.CompilerParams(vmem_limit_bytes=64 * 1024 * 1024),
    )(*results)


def solution(mesh):
    placed = (
        P("grp", "seq", None),
        P("grp", "seq", None),
        P("grp", "seq", None),
        P("grp", "seq"),
        P("grp", "seq"),
        P("grp", "seq", None),
        P(),
    )
    return jax.shard_map(
        shards,
        mesh=mesh,
        in_specs=placed,
        out_specs=(P("grp", "seq", None), P("grp", "seq", None), P("grp", "seq", None)),
        check_vma=False,
    )
```

```python
import math

import jax
import jax.numpy as jnp
from jax import lax
from jax.experimental import pallas as pl
from jax.experimental.pallas import tpu as pltpu
from jax.sharding import PartitionSpec as P

XN = 4
ZN = 8
CN = 2
GN = 4
H = 5
DH = 128
TOK = 128
PTOK = 64
ROWS = H * TOK
UNIT = 512
SPAN = 4096
SCALE = 1.0 / math.sqrt(DH)
C2 = SCALE * 1.4426950408889634
NEG = -1e30
MESH = pl.DeviceIdType.MESH
N_SEM = 112

COMP_AT = [1, 7, 2, 6, 3, 5, 4, 0]
PROMPT_AT = [0, 1, 7, 2, 6, 3, 5, 4]
PAIRS = [(1, 3), (0, 2)]
WIDE = 2 * ROWS


def token_slot(i):
    for p, pair in enumerate(PAIRS):
        if i in pair:
            return p, pair.index(i) * ROWS


def comp_slot(o):
    at = COMP_AT.index(o)
    return at // 2, (at % 2) * CN * TOK


def prompt_slot(o):
    at = PROMPT_AT.index(o)
    return 4 + at // 4, (at % 4) * CN * PTOK


def nt(a, b):
    return lax.dot_general(a, b, (((1,), (1,)), ((), ())), preferred_element_type=jnp.float32)


def nn(a, b):
    return lax.dot_general(a, b, (((1,), (0,)), ((), ())), preferred_element_type=jnp.float32)


def tn(a, b):
    return lax.dot_general(a, b, (((0,), (0,)), ((), ())), preferred_element_type=jnp.float32)


def kernel(
    owned,
    ids,
    pos,
    q_in,
    d_in,
    kv_in,
    p_in,
    dq_out,
    dc_out,
    dp_out,
    code,
    gq,
    gd,
    gqc,
    gkc,
    keys,
    wide,
    qs,
    ds,
    slots,
    mine,
    st,
    sbuf,
    norm,
    logit,
    second,
    acc,
    dqt,
    own_c,
    own_p,
    pair_s,
    pair_r,
    zs,
    zin_c,
    zin_p,
    via_c,
    via_c4,
    via_p,
    via_p4,
    dqs,
    dqr,
    yslots,
    send,
    recv,
    loc,
):
    f32, bf = jnp.float32, jnp.bfloat16
    s_at = lax.axis_index("seq")
    g = lax.axis_index("grp")
    x, z, c = s_at // (ZN * CN), lax.rem(s_at // CN, ZN), lax.rem(s_at, CN)

    def dev(dx, dz, dc, dg=0):
        xx, zz, gg = lax.rem(x + dx, XN), lax.rem(z + dz, ZN), lax.rem(g + dg, GN)
        cc = 1 - c if dc else c
        return (xx * (ZN * CN) + zz * CN + cc, gg)

    everyone = []
    count = [0]

    def start(src, dst, to):
        cp = pltpu.make_async_remote_copy(
            src_ref=src,
            dst_ref=dst,
            send_sem=send.at[count[0]],
            recv_sem=recv.at[count[0]],
            device_id=to,
            device_id_type=MESH,
        )
        count[0] += 1
        cp.start()
        everyone.append(cp)
        return cp

    def got(*cps):
        for cp in cps:
            cp.wait_recv()

    local_n = [0]

    def local(src, dst):
        cp = pltpu.make_async_copy(src, dst, loc.at[local_n[0]])
        local_n[0] += 1
        cp.start()
        return cp

    def comp_rows(o, other, lo=0, n=TOK):
        u, r = comp_slot(o)
        return keys.at[u, pl.ds(r + other * TOK + lo, n)]

    def prompt_rows(o, other, lo=0, n=PTOK):
        u, r = prompt_slot(o)
        return keys.at[u, pl.ds(r + other * PTOK + lo, n)]

    def code_row(o, other):
        u, r = comp_slot(o)
        return gkc.at[u * 4 + r // TOK + other]

    l_q = local(q_in, gq.at[0])
    l_d = local(d_in, gd.at[0])
    l_kv = local(kv_in, comp_rows(0, 0))
    l_p = local(p_in, slots.at[0])
    code[...] = jnp.broadcast_to(ids[...] * SPAN + pos[...], (8, TOK))
    gqc[0] = code[...]
    u0, r0 = comp_slot(0)
    gkc[u0 * 4 + r0 // TOK] = code[...]

    peer = dev(0, 0, 1)
    barrier = pltpu.get_barrier_semaphore()
    friends = [dev(i, 0, 0) for i in range(1, XN)] + [dev(0, 0, 0, i) for i in range(1, GN)]
    friends += [dev(0, i, 0) for i in range(1, ZN)] + [dev(0, i, 1) for i in range(ZN)]
    for to in friends:
        pl.semaphore_signal(barrier, inc=1, device_id=to, device_id_type=MESH)
    acc[...] = jnp.zeros_like(acc)
    dqt[...] = jnp.zeros_like(dqt)
    for p in range(2):
        st[p, 0:1, :] = jnp.full((1, WIDE), NEG, f32)
        st[p, 1:8, :] = jnp.zeros((7, WIDE), f32)
    for cp in (l_p, l_kv, l_q, l_d):
        cp.wait()
    pl.semaphore_wait(barrier, len(friends))

    y_cps = [start(slots.at[0], slots.at[GN - i], dev(0, 0, 0, i)) for i in range(1, GN)]
    code_cps = [start(code, code_row(0, 1), peer)]
    for i in range(1, ZN):
        code_cps.append(start(code, code_row(ZN - i, 0), dev(0, i, 0)))
        code_cps.append(start(code, code_row(ZN - i, 1), dev(0, i, 1)))
    for i in range(1, XN):
        code_cps.append(start(code, gqc.at[XN - i], dev(i, 0, 0)))
    k_cps, r_cps, p_cps, rp_cps, xq, xd = {}, {}, {}, {}, {}, {}
    mine_k = comp_rows(0, 0)
    xq[3] = start(gq.at[0], gq.at[3], dev(1, 0, 0))
    xd[1] = start(gd.at[0], gd.at[1], dev(3, 0, 0))
    for i in (1, 7):
        k_cps[8 - i] = start(mine_k, comp_rows(8 - i, 0), dev(0, i, 0))
    r_cps[0] = start(mine_k, comp_rows(0, 1), peer)
    for i in (2, 6):
        k_cps[8 - i] = start(mine_k, comp_rows(8 - i, 0), dev(0, i, 0))
    xd[3] = start(gd.at[0], gd.at[3], dev(1, 0, 0))
    xq[1] = start(gq.at[0], gq.at[1], dev(3, 0, 0))

    def relay(*os):
        for o in os:
            r_cps[o] = start(comp_rows(o, 0), comp_rows(o, 1), peer)

    def relay_p(*os):
        for o in os:
            rp_cps[o] = start(prompt_rows(o, 0), prompt_rows(o, 1), peer)

    def loop(n, body):
        def step(j, _):
            body(j)
            return 0

        lax.fori_loop(0, n, step, 0)

    def widen(j):
        wide[j // 4, pl.ds(pl.multiple_of(lax.rem(j, 4) * TOK, TOK), TOK), :] = jnp.broadcast_to(
            gkc[j, 0:1, :], (TOK, TOK)
        ).T

    def spread(i):
        p, at = token_slot(i)
        for h in range(H):
            rows = slice(at + h * TOK, at + (h + 1) * TOK)
            qs[p, rows, :] = gq[i, :, h * DH : (h + 1) * DH]
            ds[p, rows, :] = gd[i, :, h * DH : (h + 1) * DH]

    def visible(u, p, half):
        masks = []
        for i in PAIRS[p] if half is None else [PAIRS[p][half]]:
            qc = gqc[i, 0:1, :]
            kc = wide[u]
            base = qc - jnp.bitwise_and(qc, SPAN - 1)
            masks += [(kc <= qc) & (kc >= base)] * H
        return jnp.concatenate(masks, 1)

    def stat_tile(u, p, masked, half=None):
        at = slice(0, WIDE) if half is None else slice(half * ROWS, (half + 1) * ROWS)
        k = keys[u]
        s = nt(k[:, :DH], qs[p, at])
        if masked:
            s = jnp.where(visible(u, p, half), s, NEG)
        s = s * C2
        logit[u, p, :, at] = s
        dp = nt(k[:, DH:], ds[p, at])
        if not masked:
            second[u - 4, p] = dp
        m = st[p, 0:1, at]
        m2 = jnp.maximum(m, jnp.max(s, 0, keepdims=True))
        e = jnp.exp2(s - m2)
        a = jnp.exp2(m - m2)
        st[p, 0:1, at] = m2
        st[p, 1:2, at] = st[p, 1:2, at] * a + jnp.sum(e, 0, keepdims=True)
        st[p, 2:3, at] = st[p, 2:3, at] * a + jnp.sum(e * dp, 0, keepdims=True)

    spread(0)
    got(*y_cps)
    total = jnp.zeros((PTOK, 2 * DH), f32)
    for i in range(GN):
        w = (owned[lax.rem(g + i, GN)] == g).astype(f32)
        total = total + slots[i].astype(f32) * w
    mine[...] = total.astype(bf)
    for i in (1, 7, 2, 6):
        p_cps[8 - i] = start(mine, prompt_rows(8 - i, 0), dev(0, i, 0))
    rp_cps[0] = start(mine, prompt_rows(0, 1), peer)
    u, r = prompt_slot(0)
    keys[u, r : r + PTOK, :] = mine[...]
    got(k_cps[1], k_cps[7])
    relay(1, 7)
    got(*code_cps)
    loop(4 * 4, widen)
    half, phalf = TOK // 2, PTOK // 2
    got(k_cps[2], k_cps[6])
    k_cps[5] = start(comp_rows(6, 0), comp_rows(5, 0), dev(0, 1, 0))
    k_cps[3] = start(comp_rows(2, 0), comp_rows(3, 0), dev(0, 7, 0))
    far = [
        start(comp_rows(6, 0, 0, half), comp_rows(4, 0, 0, half), dev(0, 2, 0)),
        start(comp_rows(2, 0, half, half), comp_rows(4, 0, half, half), dev(0, 6, 0)),
    ]
    relay(2, 6)
    got(xq[3])
    xq[2] = start(gq.at[3], gq.at[2], dev(1, 0, 0))
    got(xd[1])
    xd[2] = start(gd.at[1], gd.at[2], dev(3, 0, 0))
    got(r_cps[1], r_cps[7])
    stat_tile(0, 1, True, 0)
    got(r_cps[2], r_cps[6])
    stat_tile(1, 1, True, 0)
    got(xd[3], xq[1])
    spread(1)
    spread(3)
    stat_tile(0, 0, True)
    got(p_cps[1], p_cps[7], p_cps[2], p_cps[6])
    p_cps[5] = start(prompt_rows(6, 0), prompt_rows(5, 0), dev(0, 1, 0))
    p_cps[3] = start(prompt_rows(2, 0), prompt_rows(3, 0), dev(0, 7, 0))
    pfar = [
        start(prompt_rows(6, 0, 0, phalf), prompt_rows(4, 0, 0, phalf), dev(0, 2, 0)),
        start(prompt_rows(2, 0, phalf, phalf), prompt_rows(4, 0, phalf, phalf), dev(0, 6, 0)),
    ]
    relay_p(1, 7, 2, 6)
    got(k_cps[3], k_cps[5], *far)
    relay(3, 5, 4)
    stat_tile(1, 0, True)
    got(r_cps[0], r_cps[3], r_cps[5], r_cps[4])
    loop(2, lambda u: stat_tile(2 + u, 0, True))
    got(xq[2], xd[2])
    spread(2)
    loop(2, lambda u: stat_tile(u, 1, True, 1))
    loop(2, lambda u: stat_tile(2 + u, 1, True))
    got(p_cps[3], p_cps[5], *pfar)
    relay_p(3, 5, 4)
    got(rp_cps[0], rp_cps[1], rp_cps[7], rp_cps[2])
    got(rp_cps[6], rp_cps[3], rp_cps[5], rp_cps[4])
    loop(2, lambda u: stat_tile(4 + u, 0, False))
    st_cps = []

    def share(i):
        p, at = token_slot(i)
        for j in range(1, XN):
            p2, at2 = token_slot((i - j) % XN)
            to = sbuf.at[XN - 1 - j, p2, :, pl.ds(at2, ROWS)]
            st_cps.append(start(st.at[p, :, pl.ds(at, ROWS)], to, dev(j, 0, 0)))

    share(1)
    share(3)
    loop(2, lambda u: stat_tile(4 + u, 1, False))
    share(0)
    share(2)
    got(*st_cps)
    for i in range(2):
        parts = [st[i]] + [sbuf[j, i] for j in range(XN - 1)]
        m = parts[0][0:1]
        for p in parts[1:]:
            m = jnp.maximum(m, p[0:1])
        l = jnp.zeros_like(m)
        w = jnp.zeros_like(m)
        for p in parts:
            a = jnp.exp2(p[0:1] - m)
            l = l + p[1:2] * a
            w = w + p[2:3] * a
        norm[i, 0:1, :] = m + jnp.log2(l)
        norm[i, 1:2, :] = w / l

    def grad_tile(e, u, i, lo=0, n=UNIT):
        kk = keys[u, lo : lo + n]
        qrow, drow = qs[i], ds[i]
        p = jnp.exp2(logit[u, i, lo : lo + n] - norm[i, 0:1, :])
        dp = second[u - 4, i] if u >= 4 else nt(kk[:, DH:], drow)
        dl = (p * (dp - norm[i, 1:2, :])).astype(bf)
        acc[e, :n, :DH] += nn(dl, qrow)
        acc[e, :n, DH:] += nn(p.astype(bf), drow)
        dqt[i] += tn(kk[:, :DH], dl)

    pair_cps, z_cps = {}, {}

    def emit(e, n, tiles):
        for t in range(tiles):
            r = (t * 2 + 1) * n
            pair_s[e, t * n : (t + 1) * n, :DH] = (acc[e, r : r + n, :DH] * SCALE).astype(bf)
            pair_s[e, t * n : (t + 1) * n, DH:] = acc[e, r : r + n, DH:].astype(bf)
        rows = pl.ds(0, n * tiles)
        pair_cps[e] = start(pair_s.at[e, rows], pair_r.at[e, rows], peer)

    v_cps = {}
    summed = set()

    def forward(e, n, tiles, own, zin, via, via4):
        if e not in summed:
            got(pair_cps[e])
            summed.add(e)
        half = n // 2
        for t, o in tiles:
            rows = slice(t * n, (t + 1) * n)
            mine_k = acc[e, t * 2 * n : (t * 2 + 1) * n, :DH] * SCALE
            mine_v = acc[e, t * 2 * n : (t * 2 + 1) * n, DH:]
            both = jnp.concatenate([mine_k, mine_v], 1) + pair_r[e, rows, :].astype(f32)
            if o == 0:
                own[...] = both
                continue
            if o in (2, 6):
                w = 0 if o == 2 else 1
                got(v_cps[(n, 3 + 2 * w)], v_cps[(n, 4, w)])
                extra = via4[w].astype(f32)
                none = jnp.zeros_like(extra)
                extra = jnp.concatenate([none, extra] if w else [extra, none], 0)
                both = both + via[w].astype(f32) + extra
            zs[e, rows, :] = both.astype(bf)
            src = zs.at[e, pl.ds(t * n, n)]
            if o == 3:
                v_cps[(n, 3)] = start(src, via.at[0], dev(0, 1, 0))
            elif o == 5:
                v_cps[(n, 5)] = start(src, via.at[1], dev(0, 7, 0))
            elif o == 4:
                v_cps[(n, 4, 0)] = start(zs.at[e, pl.ds(t * n, half)], via4.at[0], dev(0, 2, 0))
                v_cps[(n, 4, 1)] = start(zs.at[e, pl.ds(t * n + half, half)], via4.at[1], dev(0, 6, 0))
            else:
                z_cps[(e, o)] = start(src, zin.at[ZN - 1 - o], dev(0, o, 0))

    def forward_p(e, *tiles):
        forward(e, PTOK, tiles, own_p, zin_p, via_p, via_p4)

    def forward_c(e, *tiles):
        forward(e, TOK, tiles, own_c, zin_c, via_c, via_c4)

    dq_cps = []

    def put_query(i):
        p, at = token_slot(i)
        for h in range(H):
            part = dqt[p, :, at + h * TOK : at + (h + 1) * TOK].T * SCALE
            dqs[i, :, h * DH : (h + 1) * DH] = part.astype(bf)
        if i:
            dq_cps.append(start(dqs.at[i], dqr.at[XN - 1 - i], dev(i, 0, 0)))

    loop(2, lambda i: grad_tile(5, 5, i))
    emit(5, PTOK, 4)
    loop(2, lambda i: grad_tile(4, 4, i))
    emit(4, PTOK, 4)
    forward_p(5, (1, 3), (2, 5), (3, 4))
    loop(2, lambda i: grad_tile(3, 3, i, 0, UNIT // 2))
    emit(3, TOK, 1)
    forward_p(4, (0, 0), (1, 1), (2, 7))
    loop(2, lambda i: grad_tile(2, 2, i))
    emit(2, TOK, 2)
    forward_c(3, (0, 4))
    forward_p(4, (3, 2))
    forward_p(5, (0, 6))
    loop(2, lambda i: grad_tile(1, 1, i))
    emit(1, TOK, 2)
    forward_c(2, (0, 3), (1, 5))
    grad_tile(0, 0, 1)
    grad_tile(6, 3, 1, UNIT // 2, UNIT // 2)
    put_query(2)
    put_query(0)
    forward_c(1, (0, 2), (1, 6))
    got(*[cp for (e, o), cp in z_cps.items() if e in (4, 5)])
    total = own_p[...]
    for j in (0, 1, 5, 6):
        total = total + zin_p[j].astype(f32)
    yslots[0] = total.astype(bf)
    my_cps = [start(yslots.at[0], yslots.at[GN - j], dev(0, 0, 0, j)) for j in range(1, GN)]
    grad_tile(0, 0, 0)
    emit(0, TOK, 2)
    grad_tile(6, 3, 0, UNIT // 2, UNIT // 2)
    emit(6, TOK, 1)
    put_query(1)
    put_query(3)
    forward_c(0, (0, 1), (1, 7))
    forward_c(6, (0, 0))
    got(*my_cps)
    total = jnp.zeros((PTOK, 2 * DH), f32)
    wanted = owned[g]
    for i in range(GN):
        w = (wanted == lax.rem(g + i, GN)).astype(f32)
        total = total + yslots[i].astype(f32) * w
    dp_out[...] = total.astype(bf)
    got(*dq_cps)
    total = dqs[0].astype(f32)
    for j in range(XN - 1):
        total = total + dqr[j].astype(f32)
    dq_out[...] = total.astype(bf)
    got(*[cp for (e, o), cp in z_cps.items() if e not in (4, 5)])
    total = own_c[...]
    for j in (0, 1, 5, 6):
        total = total + zin_c[j].astype(f32)
    dc_out[...] = total.astype(bf)
    for cp in everyone:
        cp.wait_send()


def shards(queries, comp_kv, out_grad, comp_ids, comp_pos, prompt_kv, owned_prompt):
    bf, f32, i32 = jnp.bfloat16, jnp.float32, jnp.int32
    hbm = pl.BlockSpec(memory_space=pl.ANY)
    vmem = pl.BlockSpec(memory_space=pltpu.VMEM)
    smem = pl.BlockSpec(memory_space=pltpu.SMEM)
    grad_q, grad_c, grad_p = pl.pallas_call(
        kernel,
        out_shape=[
            jax.ShapeDtypeStruct((TOK, ROWS), bf),
            jax.ShapeDtypeStruct((TOK, 2 * DH), bf),
            jax.ShapeDtypeStruct((PTOK, 2 * DH), bf),
        ],
        in_specs=[smem, vmem, vmem] + [hbm] * 4,
        out_specs=[vmem] * 3,
        scratch_shapes=[
            pltpu.VMEM((8, TOK), i32),
            pltpu.VMEM((XN, TOK, ROWS), bf),
            pltpu.VMEM((XN, TOK, ROWS), bf),
            pltpu.VMEM((XN, 8, TOK), i32),
            pltpu.VMEM((16, 8, TOK), i32),
            pltpu.VMEM((6, UNIT, 2 * DH), bf),
            pltpu.VMEM((4, UNIT, TOK), i32),
            pltpu.VMEM((2, WIDE, DH), bf),
            pltpu.VMEM((2, WIDE, DH), bf),
            pltpu.VMEM((GN, PTOK, 2 * DH), bf),
            pltpu.VMEM((PTOK, 2 * DH), bf),
            pltpu.VMEM((2, 8, WIDE), f32),
            pltpu.VMEM((XN - 1, 2, 8, WIDE), f32),
            pltpu.VMEM((2, 8, WIDE), f32),
            pltpu.VMEM((6, 2, UNIT, WIDE), f32),
            pltpu.VMEM((2, 2, UNIT, WIDE), f32),
            pltpu.VMEM((7, UNIT, 2 * DH), f32),
            pltpu.VMEM((2, DH, WIDE), f32),
            pltpu.VMEM((TOK, 2 * DH), f32),
            pltpu.VMEM((PTOK, 2 * DH), f32),
            pltpu.VMEM((7, UNIT // 2, 2 * DH), bf),
            pltpu.VMEM((7, UNIT // 2, 2 * DH), bf),
            pltpu.VMEM((7, UNIT // 2, 2 * DH), bf),
            pltpu.VMEM((ZN - 1, TOK, 2 * DH), bf),
            pltpu.VMEM((ZN - 1, PTOK, 2 * DH), bf),
            pltpu.VMEM((2, TOK, 2 * DH), bf),
            pltpu.VMEM((2, TOK // 2, 2 * DH), bf),
            pltpu.VMEM((2, PTOK, 2 * DH), bf),
            pltpu.VMEM((2, PTOK // 2, 2 * DH), bf),
            pltpu.VMEM((XN, TOK, ROWS), bf),
            pltpu.VMEM((XN - 1, TOK, ROWS), bf),
            pltpu.VMEM((GN, PTOK, 2 * DH), bf),
            pltpu.SemaphoreType.DMA((N_SEM,)),
            pltpu.SemaphoreType.DMA((N_SEM,)),
            pltpu.SemaphoreType.DMA((4,)),
        ],
        compiler_params=pltpu.CompilerParams(
            collective_id=0, has_side_effects=True, vmem_limit_bytes=64 * 1024 * 1024
        ),
    )(owned_prompt, comp_ids, comp_pos, queries[0], out_grad[0], comp_kv[0], prompt_kv[0])
    return grad_q[None], grad_c[None], grad_p[None]


def solution(mesh):
    placed = (
        P("grp", "seq", None),
        P("grp", "seq", None),
        P("grp", "seq", None),
        P("grp", "seq"),
        P("grp", "seq"),
        P("grp", "seq", None),
        P(),
    )
    return jax.shard_map(
        shards,
        mesh=mesh,
        in_specs=placed,
        out_specs=(P("grp", "seq", None), P("grp", "seq", None), P("grp", "seq", None)),
        check_vma=False,
    )
```

```python
import math

import jax
import jax.numpy as jnp
from jax import lax
from jax.experimental import pallas as pl
from jax.experimental.pallas import tpu as pltpu
from jax.sharding import PartitionSpec as P

XN = 4
ZN = 8
CN = 2
GN = 4
H = 5
DH = 128
TOK = 128
PTOK = 64
ROWS = H * TOK
UNIT = 512
SPAN = 4096
SCALE = 1.0 / math.sqrt(DH)
C2 = SCALE * 1.4426950408889634
NEG = -1e30
MESH = pl.DeviceIdType.MESH
N_SEM = 112

COMP_AT = [1, 7, 2, 6, 3, 5, 4, 0]
PROMPT_AT = [0, 1, 7, 2, 6, 3, 5, 4]
PAIRS = [(1, 3), (0, 2)]
WIDE = 2 * ROWS


def token_slot(i):
    for p, pair in enumerate(PAIRS):
        if i in pair:
            return p, pair.index(i) * ROWS


def comp_slot(o):
    at = COMP_AT.index(o)
    return at // 2, (at % 2) * CN * TOK


def prompt_slot(o):
    at = PROMPT_AT.index(o)
    return 4 + at // 4, (at % 4) * CN * PTOK


def nt(a, b):
    return lax.dot_general(a, b, (((1,), (1,)), ((), ())), preferred_element_type=jnp.float32)


def nn(a, b):
    return lax.dot_general(a, b, (((1,), (0,)), ((), ())), preferred_element_type=jnp.float32)


def tn(a, b):
    return lax.dot_general(a, b, (((0,), (0,)), ((), ())), preferred_element_type=jnp.float32)


def kernel(
    owned,
    ids,
    pos,
    q_in,
    d_in,
    kv_in,
    p_in,
    dq_out,
    dc_out,
    dp_out,
    code,
    gq,
    gd,
    gqc,
    gkc,
    keys,
    wide,
    qs,
    ds,
    slots,
    mine,
    st,
    sbuf,
    norm,
    logit,
    second,
    acc,
    dqt,
    own_c,
    own_p,
    pair_s,
    pair_r,
    zs,
    zin_c,
    zin_p,
    via_c,
    via_c4,
    via_p,
    via_p4,
    dqs,
    dqr,
    yslots,
    send,
    recv,
    loc,
):
    f32, bf = jnp.float32, jnp.bfloat16
    s_at = lax.axis_index("seq")
    g = lax.axis_index("grp")
    x, z, c = s_at // (ZN * CN), lax.rem(s_at // CN, ZN), lax.rem(s_at, CN)

    def dev(dx, dz, dc, dg=0):
        xx, zz, gg = lax.rem(x + dx, XN), lax.rem(z + dz, ZN), lax.rem(g + dg, GN)
        cc = 1 - c if dc else c
        return (xx * (ZN * CN) + zz * CN + cc, gg)

    everyone = []
    count = [0]

    def start(src, dst, to):
        cp = pltpu.make_async_remote_copy(
            src_ref=src,
            dst_ref=dst,
            send_sem=send.at[count[0]],
            recv_sem=recv.at[count[0]],
            device_id=to,
            device_id_type=MESH,
        )
        count[0] += 1
        cp.start()
        everyone.append(cp)
        return cp

    def got(*cps):
        for cp in cps:
            cp.wait_recv()

    local_n = [0]

    def local(src, dst):
        cp = pltpu.make_async_copy(src, dst, loc.at[local_n[0]])
        local_n[0] += 1
        cp.start()
        return cp

    def comp_rows(o, other, lo=0, n=TOK):
        u, r = comp_slot(o)
        return keys.at[u, pl.ds(r + other * TOK + lo, n)]

    def prompt_rows(o, other, lo=0, n=PTOK):
        u, r = prompt_slot(o)
        return keys.at[u, pl.ds(r + other * PTOK + lo, n)]

    def code_row(o, other):
        u, r = comp_slot(o)
        return gkc.at[u * 4 + r // TOK + other]

    l_q = local(q_in, gq.at[0])
    l_d = local(d_in, gd.at[0])
    l_kv = local(kv_in, comp_rows(0, 0))
    l_p = local(p_in, slots.at[0])
    code[...] = jnp.broadcast_to(ids[...] * SPAN + pos[...], (8, TOK))
    gqc[0] = code[...]
    u0, r0 = comp_slot(0)
    gkc[u0 * 4 + r0 // TOK] = code[...]

    peer = dev(0, 0, 1)
    barrier = pltpu.get_barrier_semaphore()
    friends = [dev(i, 0, 0) for i in range(1, XN)] + [dev(0, 0, 0, i) for i in range(1, GN)]
    friends += [dev(0, i, 0) for i in range(1, ZN)] + [dev(0, i, 1) for i in range(ZN)]
    for to in friends:
        pl.semaphore_signal(barrier, inc=1, device_id=to, device_id_type=MESH)
    acc[...] = jnp.zeros_like(acc)
    dqt[...] = jnp.zeros_like(dqt)
    for p in range(2):
        st[p, 0:1, :] = jnp.full((1, WIDE), NEG, f32)
        st[p, 1:8, :] = jnp.zeros((7, WIDE), f32)
    for cp in (l_p, l_kv, l_q, l_d):
        cp.wait()
    pl.semaphore_wait(barrier, len(friends))

    y_cps = [start(slots.at[0], slots.at[GN - i], dev(0, 0, 0, i)) for i in range(1, GN)]
    code_cps = [start(code, code_row(0, 1), peer)]
    for i in range(1, ZN):
        code_cps.append(start(code, code_row(ZN - i, 0), dev(0, i, 0)))
        code_cps.append(start(code, code_row(ZN - i, 1), dev(0, i, 1)))
    for i in range(1, XN):
        code_cps.append(start(code, gqc.at[XN - i], dev(i, 0, 0)))
    k_cps, r_cps, p_cps, rp_cps, xq, xd = {}, {}, {}, {}, {}, {}
    mine_k = comp_rows(0, 0)
    xq[3] = start(gq.at[0], gq.at[3], dev(1, 0, 0))
    xd[1] = start(gd.at[0], gd.at[1], dev(3, 0, 0))
    for i in (1, 7):
        k_cps[8 - i] = start(mine_k, comp_rows(8 - i, 0), dev(0, i, 0))
    r_cps[0] = start(mine_k, comp_rows(0, 1), peer)
    for i in (2, 6):
        k_cps[8 - i] = start(mine_k, comp_rows(8 - i, 0), dev(0, i, 0))
    xd[3] = start(gd.at[0], gd.at[3], dev(1, 0, 0))
    xq[1] = start(gq.at[0], gq.at[1], dev(3, 0, 0))

    def relay(*os):
        for o in os:
            r_cps[o] = start(comp_rows(o, 0), comp_rows(o, 1), peer)

    def relay_p(*os):
        for o in os:
            rp_cps[o] = start(prompt_rows(o, 0), prompt_rows(o, 1), peer)

    def loop(n, body):
        def step(j, _):
            body(j)
            return 0

        lax.fori_loop(0, n, step, 0)

    def widen(j):
        wide[j // 4, pl.ds(pl.multiple_of(lax.rem(j, 4) * TOK, TOK), TOK), :] = jnp.broadcast_to(
            gkc[j, 0:1, :], (TOK, TOK)
        ).T

    def spread(i):
        p, at = token_slot(i)
        for h in range(H):
            rows = slice(at + h * TOK, at + (h + 1) * TOK)
            qs[p, rows, :] = gq[i, :, h * DH : (h + 1) * DH]
            ds[p, rows, :] = gd[i, :, h * DH : (h + 1) * DH]

    def visible(u, p, half):
        masks = []
        for i in PAIRS[p] if half is None else [PAIRS[p][half]]:
            qc = gqc[i, 0:1, :]
            kc = wide[u]
            base = qc - jnp.bitwise_and(qc, SPAN - 1)
            masks += [(kc <= qc) & (kc >= base)] * H
        return jnp.concatenate(masks, 1)

    def stat_tile(u, p, masked, half=None):
        at = slice(0, WIDE) if half is None else slice(half * ROWS, (half + 1) * ROWS)
        k = keys[u]
        s = nt(k[:, :DH], qs[p, at])
        if masked:
            s = jnp.where(visible(u, p, half), s, NEG)
        s = s * C2
        logit[u, p, :, at] = s
        dp = nt(k[:, DH:], ds[p, at])
        if not masked:
            second[u - 4, p] = dp
        m = st[p, 0:1, at]
        m2 = jnp.maximum(m, jnp.max(s, 0, keepdims=True))
        e = jnp.exp2(s - m2)
        a = jnp.exp2(m - m2)
        st[p, 0:1, at] = m2
        st[p, 1:2, at] = st[p, 1:2, at] * a + jnp.sum(e, 0, keepdims=True)
        st[p, 2:3, at] = st[p, 2:3, at] * a + jnp.sum(e * dp, 0, keepdims=True)

    spread(0)
    got(*y_cps)
    total = jnp.zeros((PTOK, 2 * DH), f32)
    for i in range(GN):
        w = (owned[lax.rem(g + i, GN)] == g).astype(f32)
        total = total + slots[i].astype(f32) * w
    mine[...] = total.astype(bf)
    for i in (1, 7, 2, 6):
        p_cps[8 - i] = start(mine, prompt_rows(8 - i, 0), dev(0, i, 0))
    rp_cps[0] = start(mine, prompt_rows(0, 1), peer)
    u, r = prompt_slot(0)
    keys[u, r : r + PTOK, :] = mine[...]
    got(k_cps[1], k_cps[7])
    relay(1, 7)
    got(*code_cps)
    loop(4 * 4, widen)
    half, phalf = TOK // 2, PTOK // 2
    got(k_cps[2], k_cps[6])
    k_cps[5] = start(comp_rows(6, 0), comp_rows(5, 0), dev(0, 1, 0))
    k_cps[3] = start(comp_rows(2, 0), comp_rows(3, 0), dev(0, 7, 0))
    far = [
        start(comp_rows(6, 0, 0, half), comp_rows(4, 0, 0, half), dev(0, 2, 0)),
        start(comp_rows(2, 0, half, half), comp_rows(4, 0, half, half), dev(0, 6, 0)),
    ]
    relay(2, 6)
    got(xq[3])
    xq[2] = start(gq.at[3], gq.at[2], dev(1, 0, 0))
    got(xd[1])
    xd[2] = start(gd.at[1], gd.at[2], dev(3, 0, 0))
    got(r_cps[1], r_cps[7])
    stat_tile(0, 1, True, 0)
    got(r_cps[2], r_cps[6])
    stat_tile(1, 1, True, 0)
    got(xd[3], xq[1])
    spread(1)
    spread(3)
    stat_tile(0, 0, True)
    got(p_cps[1], p_cps[7], p_cps[2], p_cps[6])
    p_cps[5] = start(prompt_rows(6, 0), prompt_rows(5, 0), dev(0, 1, 0))
    p_cps[3] = start(prompt_rows(2, 0), prompt_rows(3, 0), dev(0, 7, 0))
    pfar = [
        start(prompt_rows(6, 0, 0, phalf), prompt_rows(4, 0, 0, phalf), dev(0, 2, 0)),
        start(prompt_rows(2, 0, phalf, phalf), prompt_rows(4, 0, phalf, phalf), dev(0, 6, 0)),
    ]
    relay_p(1, 7, 2, 6)
    got(k_cps[3], k_cps[5], *far)
    relay(3, 5, 4)
    stat_tile(1, 0, True)
    got(r_cps[0], r_cps[3], r_cps[5], r_cps[4])
    loop(2, lambda u: stat_tile(2 + u, 0, True))
    got(xq[2], xd[2])
    spread(2)
    loop(2, lambda u: stat_tile(u, 1, True, 1))
    loop(2, lambda u: stat_tile(2 + u, 1, True))
    got(p_cps[3], p_cps[5], *pfar)
    relay_p(3, 5, 4)
    got(rp_cps[0], rp_cps[1], rp_cps[7], rp_cps[2])
    got(rp_cps[6], rp_cps[3], rp_cps[5], rp_cps[4])
    loop(2, lambda u: stat_tile(4 + u, 0, False))
    st_cps = []

    def share(i):
        p, at = token_slot(i)
        for j in range(1, XN):
            p2, at2 = token_slot((i - j) % XN)
            to = sbuf.at[XN - 1 - j, p2, :, pl.ds(at2, ROWS)]
            st_cps.append(start(st.at[p, :, pl.ds(at, ROWS)], to, dev(j, 0, 0)))

    share(1)
    share(3)
    loop(2, lambda u: stat_tile(4 + u, 1, False))
    share(0)
    share(2)
    got(*st_cps)
    for i in range(2):
        parts = [st[i]] + [sbuf[j, i] for j in range(XN - 1)]
        m = parts[0][0:1]
        for p in parts[1:]:
            m = jnp.maximum(m, p[0:1])
        l = jnp.zeros_like(m)
        w = jnp.zeros_like(m)
        for p in parts:
            a = jnp.exp2(p[0:1] - m)
            l = l + p[1:2] * a
            w = w + p[2:3] * a
        norm[i, 0:1, :] = m + jnp.log2(l)
        norm[i, 1:2, :] = w / l

    def grad_tile(e, u, i, lo=0, n=UNIT):
        kk = keys[u, lo : lo + n]
        qrow, drow = qs[i], ds[i]
        p = jnp.exp2(logit[u, i, lo : lo + n] - norm[i, 0:1, :])
        dp = second[u - 4, i] if u >= 4 else nt(kk[:, DH:], drow)
        dl = (p * (dp - norm[i, 1:2, :])).astype(bf)
        acc[e, :n, :DH] += nn(dl, qrow)
        acc[e, :n, DH:] += nn(p.astype(bf), drow)
        dqt[i] += tn(kk[:, :DH], dl)

    pair_cps, z_cps = {}, {}

    def emit(e, n, tiles):
        for t in range(tiles):
            r = (t * 2 + 1) * n
            pair_s[e, t * n : (t + 1) * n, :DH] = (acc[e, r : r + n, :DH] * SCALE).astype(bf)
            pair_s[e, t * n : (t + 1) * n, DH:] = acc[e, r : r + n, DH:].astype(bf)
        rows = pl.ds(0, n * tiles)
        pair_cps[e] = start(pair_s.at[e, rows], pair_r.at[e, rows], peer)

    v_cps = {}
    summed = set()

    def forward(e, n, tiles, own, zin, via, via4):
        if e not in summed:
            got(pair_cps[e])
            summed.add(e)
        half = n // 2
        for t, o in tiles:
            rows = slice(t * n, (t + 1) * n)
            mine_k = acc[e, t * 2 * n : (t * 2 + 1) * n, :DH] * SCALE
            mine_v = acc[e, t * 2 * n : (t * 2 + 1) * n, DH:]
            both = jnp.concatenate([mine_k, mine_v], 1) + pair_r[e, rows, :].astype(f32)
            if o == 0:
                own[...] = both
                continue
            if o in (2, 6):
                w = 0 if o == 2 else 1
                got(v_cps[(n, 3 + 2 * w)], v_cps[(n, 4, w)])
                extra = via4[w].astype(f32)
                none = jnp.zeros_like(extra)
                extra = jnp.concatenate([none, extra] if w else [extra, none], 0)
                both = both + via[w].astype(f32) + extra
            zs[e, rows, :] = both.astype(bf)
            src = zs.at[e, pl.ds(t * n, n)]
            if o == 3:
                v_cps[(n, 3)] = start(src, via.at[0], dev(0, 1, 0))
            elif o == 5:
                v_cps[(n, 5)] = start(src, via.at[1], dev(0, 7, 0))
            elif o == 4:
                v_cps[(n, 4, 0)] = start(zs.at[e, pl.ds(t * n, half)], via4.at[0], dev(0, 2, 0))
                v_cps[(n, 4, 1)] = start(zs.at[e, pl.ds(t * n + half, half)], via4.at[1], dev(0, 6, 0))
            else:
                z_cps[(e, o)] = start(src, zin.at[ZN - 1 - o], dev(0, o, 0))

    def forward_p(e, *tiles):
        forward(e, PTOK, tiles, own_p, zin_p, via_p, via_p4)

    def forward_c(e, *tiles):
        forward(e, TOK, tiles, own_c, zin_c, via_c, via_c4)

    dq_cps = []

    def put_query(i):
        p, at = token_slot(i)
        for h in range(H):
            part = dqt[p, :, at + h * TOK : at + (h + 1) * TOK].T * SCALE
            dqs[i, :, h * DH : (h + 1) * DH] = part.astype(bf)
        if i:
            dq_cps.append(start(dqs.at[i], dqr.at[XN - 1 - i], dev(i, 0, 0)))

    loop(2, lambda i: grad_tile(5, 5, i))
    emit(5, PTOK, 4)
    loop(2, lambda i: grad_tile(4, 4, i))
    emit(4, PTOK, 4)
    forward_p(5, (1, 3), (2, 5), (3, 4))
    loop(2, lambda i: grad_tile(3, 3, i, 0, UNIT // 2))
    emit(3, TOK, 1)
    forward_p(4, (0, 0), (1, 1), (2, 7))
    loop(2, lambda i: grad_tile(2, 2, i))
    emit(2, TOK, 2)
    forward_c(3, (0, 4))
    forward_p(4, (3, 2))
    forward_p(5, (0, 6))
    loop(2, lambda i: grad_tile(1, 1, i))
    emit(1, TOK, 2)
    forward_c(2, (0, 3), (1, 5))
    grad_tile(0, 0, 1)
    grad_tile(6, 3, 1, UNIT // 2, UNIT // 2)
    put_query(2)
    put_query(0)
    forward_c(1, (0, 2), (1, 6))
    got(*[cp for (e, o), cp in z_cps.items() if e in (4, 5)])
    total = own_p[...]
    for j in (0, 1, 5, 6):
        total = total + zin_p[j].astype(f32)
    yslots[0] = total.astype(bf)
    my_cps = [start(yslots.at[0], yslots.at[GN - j], dev(0, 0, 0, j)) for j in range(1, GN)]
    grad_tile(0, 0, 0)
    emit(0, TOK, 2)
    grad_tile(6, 3, 0, UNIT // 2, UNIT // 2)
    emit(6, TOK, 1)
    put_query(1)
    put_query(3)
    forward_c(0, (0, 1), (1, 7))
    forward_c(6, (0, 0))
    got(*my_cps)
    total = jnp.zeros((PTOK, 2 * DH), f32)
    wanted = owned[g]
    for i in range(GN):
        w = (wanted == lax.rem(g + i, GN)).astype(f32)
        total = total + yslots[i].astype(f32) * w
    dp_out[...] = total.astype(bf)
    got(*dq_cps)
    total = dqs[0].astype(f32)
    for j in range(XN - 1):
        total = total + dqr[j].astype(f32)
    dq_out[...] = total.astype(bf)
    got(*[cp for (e, o), cp in z_cps.items() if e not in (4, 5)])
    total = own_c[...]
    for j in (0, 1, 5, 6):
        total = total + zin_c[j].astype(f32)
    dc_out[...] = total.astype(bf)
    for cp in everyone:
        cp.wait_send()


def hand_over(*refs):
    for i in range(3):
        refs[3 + i][0] = refs[i][...]


def shards(queries, comp_kv, out_grad, comp_ids, comp_pos, prompt_kv, owned_prompt):
    bf, f32, i32 = jnp.bfloat16, jnp.float32, jnp.int32
    hbm = pl.BlockSpec(memory_space=pl.ANY)
    vmem = pl.BlockSpec(memory_space=pltpu.VMEM)
    smem = pl.BlockSpec(memory_space=pltpu.SMEM)
    grad_q, grad_c, grad_p = pl.pallas_call(
        kernel,
        out_shape=[
            jax.ShapeDtypeStruct((TOK, ROWS), bf),
            jax.ShapeDtypeStruct((TOK, 2 * DH), bf),
            jax.ShapeDtypeStruct((PTOK, 2 * DH), bf),
        ],
        in_specs=[smem, vmem, vmem] + [hbm] * 4,
        out_specs=[vmem] * 3,
        scratch_shapes=[
            pltpu.VMEM((8, TOK), i32),
            pltpu.VMEM((XN, TOK, ROWS), bf),
            pltpu.VMEM((XN, TOK, ROWS), bf),
            pltpu.VMEM((XN, 8, TOK), i32),
            pltpu.VMEM((16, 8, TOK), i32),
            pltpu.VMEM((6, UNIT, 2 * DH), bf),
            pltpu.VMEM((4, UNIT, TOK), i32),
            pltpu.VMEM((2, WIDE, DH), bf),
            pltpu.VMEM((2, WIDE, DH), bf),
            pltpu.VMEM((GN, PTOK, 2 * DH), bf),
            pltpu.VMEM((PTOK, 2 * DH), bf),
            pltpu.VMEM((2, 8, WIDE), f32),
            pltpu.VMEM((XN - 1, 2, 8, WIDE), f32),
            pltpu.VMEM((2, 8, WIDE), f32),
            pltpu.VMEM((6, 2, UNIT, WIDE), f32),
            pltpu.VMEM((2, 2, UNIT, WIDE), f32),
            pltpu.VMEM((7, UNIT, 2 * DH), f32),
            pltpu.VMEM((2, DH, WIDE), f32),
            pltpu.VMEM((TOK, 2 * DH), f32),
            pltpu.VMEM((PTOK, 2 * DH), f32),
            pltpu.VMEM((7, UNIT // 2, 2 * DH), bf),
            pltpu.VMEM((7, UNIT // 2, 2 * DH), bf),
            pltpu.VMEM((7, UNIT // 2, 2 * DH), bf),
            pltpu.VMEM((ZN - 1, TOK, 2 * DH), bf),
            pltpu.VMEM((ZN - 1, PTOK, 2 * DH), bf),
            pltpu.VMEM((2, TOK, 2 * DH), bf),
            pltpu.VMEM((2, TOK // 2, 2 * DH), bf),
            pltpu.VMEM((2, PTOK, 2 * DH), bf),
            pltpu.VMEM((2, PTOK // 2, 2 * DH), bf),
            pltpu.VMEM((XN, TOK, ROWS), bf),
            pltpu.VMEM((XN - 1, TOK, ROWS), bf),
            pltpu.VMEM((GN, PTOK, 2 * DH), bf),
            pltpu.SemaphoreType.DMA((N_SEM,)),
            pltpu.SemaphoreType.DMA((N_SEM,)),
            pltpu.SemaphoreType.DMA((4,)),
        ],
        compiler_params=pltpu.CompilerParams(
            collective_id=0, has_side_effects=True, vmem_limit_bytes=64 * 1024 * 1024
        ),
    )(owned_prompt, comp_ids, comp_pos, queries[0], out_grad[0], comp_kv[0], prompt_kv[0])
    results = (grad_q, grad_c, grad_p)
    return pl.pallas_call(
        hand_over,
        out_shape=[jax.ShapeDtypeStruct((1,) + r.shape, r.dtype) for r in results],
        in_specs=[vmem] * 3,
        out_specs=[vmem] * 3,
        compiler_params=pltpu.CompilerParams(vmem_limit_bytes=64 * 1024 * 1024),
    )(*results)


def solution(mesh):
    placed = (
        P("grp", "seq", None),
        P("grp", "seq", None),
        P("grp", "seq", None),
        P("grp", "seq"),
        P("grp", "seq"),
        P("grp", "seq", None),
        P(),
    )
    return jax.shard_map(
        shards,
        mesh=mesh,
        in_specs=placed,
        out_specs=(P("grp", "seq", None), P("grp", "seq", None), P("grp", "seq", None)),
        check_vma=False,
    )
```

```python
import math

import jax
import jax.numpy as jnp
from jax import lax
from jax.experimental import pallas as pl
from jax.experimental.pallas import tpu as pltpu
from jax.sharding import PartitionSpec as P

XN = 4
ZN = 8
CN = 2
GN = 4
H = 5
DH = 128
TOK = 128
PTOK = 64
ROWS = H * TOK
UNIT = 512
SPAN = 4096
SCALE = 1.0 / math.sqrt(DH)
C2 = SCALE * 1.4426950408889634
NEG = -1e30
MESH = pl.DeviceIdType.MESH
N_SEM = 112

COMP_AT = [1, 7, 2, 6, 3, 5, 4, 0]
PROMPT_AT = [0, 1, 7, 2, 6, 3, 5, 4]
PAIRS = [(1, 3), (0, 2)]
WIDE = 2 * ROWS


def token_slot(i):
    for p, pair in enumerate(PAIRS):
        if i in pair:
            return p, pair.index(i) * ROWS


def comp_slot(o):
    at = COMP_AT.index(o)
    return at // 2, (at % 2) * CN * TOK


def prompt_slot(o):
    at = PROMPT_AT.index(o)
    return 4 + at // 4, (at % 4) * CN * PTOK


def nt(a, b):
    return lax.dot_general(a, b, (((1,), (1,)), ((), ())), preferred_element_type=jnp.float32)


def nn(a, b):
    return lax.dot_general(a, b, (((1,), (0,)), ((), ())), preferred_element_type=jnp.float32)


def tn(a, b):
    return lax.dot_general(a, b, (((0,), (0,)), ((), ())), preferred_element_type=jnp.float32)


def kernel(
    owned,
    ids,
    pos,
    q_in,
    d_in,
    kv_in,
    p_in,
    dq_out,
    dc_out,
    dp_out,
    code,
    gq,
    gd,
    gqc,
    gkc,
    keys,
    wide,
    qs,
    ds,
    slots,
    mine,
    st,
    packed,
    sbuf,
    norm,
    logit,
    second,
    acc,
    dqt,
    own_c,
    own_p,
    pair_s,
    pair_r,
    zs,
    zin_c,
    zin_p,
    via_c,
    via_c4,
    via_p,
    via_p4,
    dqs,
    dqr,
    yslots,
    send,
    recv,
    loc,
):
    f32, bf = jnp.float32, jnp.bfloat16
    s_at = lax.axis_index("seq")
    g = lax.axis_index("grp")
    x, z, c = s_at // (ZN * CN), lax.rem(s_at // CN, ZN), lax.rem(s_at, CN)

    def dev(dx, dz, dc, dg=0):
        xx, zz, gg = lax.rem(x + dx, XN), lax.rem(z + dz, ZN), lax.rem(g + dg, GN)
        cc = 1 - c if dc else c
        return (xx * (ZN * CN) + zz * CN + cc, gg)

    everyone = []
    count = [0]

    def start(src, dst, to):
        cp = pltpu.make_async_remote_copy(
            src_ref=src,
            dst_ref=dst,
            send_sem=send.at[count[0]],
            recv_sem=recv.at[count[0]],
            device_id=to,
            device_id_type=MESH,
        )
        count[0] += 1
        cp.start()
        everyone.append(cp)
        return cp

    def got(*cps):
        for cp in cps:
            cp.wait_recv()

    local_n = [0]

    def local(src, dst):
        cp = pltpu.make_async_copy(src, dst, loc.at[local_n[0]])
        local_n[0] += 1
        cp.start()
        return cp

    def comp_rows(o, other, lo=0, n=TOK):
        u, r = comp_slot(o)
        return keys.at[u, pl.ds(r + other * TOK + lo, n)]

    def prompt_rows(o, other, lo=0, n=PTOK):
        u, r = prompt_slot(o)
        return keys.at[u, pl.ds(r + other * PTOK + lo, n)]

    def code_row(o, other):
        u, r = comp_slot(o)
        return gkc.at[u * 4 + r // TOK + other]

    l_q = local(q_in, gq.at[0])
    l_d = local(d_in, gd.at[0])
    l_kv = local(kv_in, comp_rows(0, 0))
    l_p = local(p_in, slots.at[0])
    code[...] = jnp.broadcast_to(ids[...] * SPAN + pos[...], (8, TOK))
    gqc[0] = code[...]
    u0, r0 = comp_slot(0)
    gkc[u0 * 4 + r0 // TOK] = code[...]

    peer = dev(0, 0, 1)
    barrier = pltpu.get_barrier_semaphore()
    friends = [dev(i, 0, 0) for i in range(1, XN)] + [dev(0, 0, 0, i) for i in range(1, GN)]
    friends += [dev(0, i, 0) for i in range(1, ZN)] + [dev(0, i, 1) for i in range(ZN)]
    for to in friends:
        pl.semaphore_signal(barrier, inc=1, device_id=to, device_id_type=MESH)
    acc[...] = jnp.zeros_like(acc)
    dqt[...] = jnp.zeros_like(dqt)
    for p in range(2):
        st[p, 0:1, :] = jnp.full((1, WIDE), NEG, f32)
        st[p, 1:8, :] = jnp.zeros((7, WIDE), f32)
    for cp in (l_p, l_kv, l_q, l_d):
        cp.wait()
    pl.semaphore_wait(barrier, len(friends))

    y_cps = [start(slots.at[0], slots.at[GN - i], dev(0, 0, 0, i)) for i in range(1, GN)]
    code_cps = [start(code, code_row(0, 1), peer)]
    for i in range(1, ZN):
        code_cps.append(start(code, code_row(ZN - i, 0), dev(0, i, 0)))
        code_cps.append(start(code, code_row(ZN - i, 1), dev(0, i, 1)))
    for i in range(1, XN):
        code_cps.append(start(code, gqc.at[XN - i], dev(i, 0, 0)))
    k_cps, r_cps, p_cps, rp_cps, xq, xd = {}, {}, {}, {}, {}, {}
    mine_k = comp_rows(0, 0)
    xq[3] = start(gq.at[0], gq.at[3], dev(1, 0, 0))
    xd[1] = start(gd.at[0], gd.at[1], dev(3, 0, 0))
    for i in (1, 7):
        k_cps[8 - i] = start(mine_k, comp_rows(8 - i, 0), dev(0, i, 0))
    r_cps[0] = start(mine_k, comp_rows(0, 1), peer)
    for i in (2, 6):
        k_cps[8 - i] = start(mine_k, comp_rows(8 - i, 0), dev(0, i, 0))
    xd[3] = start(gd.at[0], gd.at[3], dev(1, 0, 0))
    xq[1] = start(gq.at[0], gq.at[1], dev(3, 0, 0))

    def relay(*os):
        for o in os:
            r_cps[o] = start(comp_rows(o, 0), comp_rows(o, 1), peer)

    def relay_p(*os):
        for o in os:
            rp_cps[o] = start(prompt_rows(o, 0), prompt_rows(o, 1), peer)

    def loop(n, body):
        def step(j, _):
            body(j)
            return 0

        lax.fori_loop(0, n, step, 0)

    def widen(j):
        wide[j // 4, pl.ds(pl.multiple_of(lax.rem(j, 4) * TOK, TOK), TOK), :] = jnp.broadcast_to(
            gkc[j, 0:1, :], (TOK, TOK)
        ).T

    def spread(i):
        p, at = token_slot(i)
        for h in range(H):
            rows = slice(at + h * TOK, at + (h + 1) * TOK)
            qs[p, rows, :] = gq[i, :, h * DH : (h + 1) * DH]
            ds[p, rows, :] = gd[i, :, h * DH : (h + 1) * DH]

    def visible(u, p, half):
        masks = []
        for i in PAIRS[p] if half is None else [PAIRS[p][half]]:
            qc = gqc[i, 0:1, :]
            kc = wide[u]
            base = qc - jnp.bitwise_and(qc, SPAN - 1)
            masks += [(kc <= qc) & (kc >= base)] * H
        return jnp.concatenate(masks, 1)

    def stat_tile(u, p, masked, half=None):
        at = slice(0, WIDE) if half is None else slice(half * ROWS, (half + 1) * ROWS)
        k = keys[u]
        s = nt(k[:, :DH], qs[p, at])
        if masked:
            s = jnp.where(visible(u, p, half), s, NEG)
        s = s * C2
        logit[u, p, :, at] = s
        dp = nt(k[:, DH:], ds[p, at])
        if not masked:
            second[u - 4, p] = dp
        m = st[p, 0:1, at]
        m2 = jnp.maximum(m, jnp.max(s, 0, keepdims=True))
        e = jnp.exp2(s - m2)
        a = jnp.exp2(m - m2)
        st[p, 0:1, at] = m2
        st[p, 1:2, at] = st[p, 1:2, at] * a + jnp.sum(e, 0, keepdims=True)
        st[p, 2:3, at] = st[p, 2:3, at] * a + jnp.sum(e * dp, 0, keepdims=True)

    spread(0)
    got(*y_cps)
    total = jnp.zeros((PTOK, 2 * DH), f32)
    for i in range(GN):
        w = (owned[lax.rem(g + i, GN)] == g).astype(f32)
        total = total + slots[i].astype(f32) * w
    mine[...] = total.astype(bf)
    for i in (1, 7, 2, 6):
        p_cps[8 - i] = start(mine, prompt_rows(8 - i, 0), dev(0, i, 0))
    rp_cps[0] = start(mine, prompt_rows(0, 1), peer)
    u, r = prompt_slot(0)
    keys[u, r : r + PTOK, :] = mine[...]
    got(k_cps[1], k_cps[7])
    relay(1, 7)
    got(*code_cps)
    loop(4 * 4, widen)
    half, phalf = TOK // 2, PTOK // 2
    got(k_cps[2], k_cps[6])
    k_cps[5] = start(comp_rows(6, 0), comp_rows(5, 0), dev(0, 1, 0))
    k_cps[3] = start(comp_rows(2, 0), comp_rows(3, 0), dev(0, 7, 0))
    far = [
        start(comp_rows(6, 0, 0, half), comp_rows(4, 0, 0, half), dev(0, 2, 0)),
        start(comp_rows(2, 0, half, half), comp_rows(4, 0, half, half), dev(0, 6, 0)),
    ]
    relay(2, 6)
    got(xq[3])
    xq[2] = start(gq.at[3], gq.at[2], dev(1, 0, 0))
    got(xd[1])
    xd[2] = start(gd.at[1], gd.at[2], dev(3, 0, 0))
    got(r_cps[1], r_cps[7])
    stat_tile(0, 1, True, 0)
    got(r_cps[2], r_cps[6])
    stat_tile(1, 1, True, 0)
    got(xd[3], xq[1])
    spread(1)
    spread(3)
    stat_tile(0, 0, True)
    got(p_cps[1], p_cps[7], p_cps[2], p_cps[6])
    p_cps[5] = start(prompt_rows(6, 0), prompt_rows(5, 0), dev(0, 1, 0))
    p_cps[3] = start(prompt_rows(2, 0), prompt_rows(3, 0), dev(0, 7, 0))
    pfar = [
        start(prompt_rows(6, 0, 0, phalf), prompt_rows(4, 0, 0, phalf), dev(0, 2, 0)),
        start(prompt_rows(2, 0, phalf, phalf), prompt_rows(4, 0, phalf, phalf), dev(0, 6, 0)),
    ]
    relay_p(1, 7, 2, 6)
    got(k_cps[3], k_cps[5], *far)
    relay(3, 5, 4)
    stat_tile(1, 0, True)
    got(r_cps[0], r_cps[3], r_cps[5], r_cps[4])
    loop(2, lambda u: stat_tile(2 + u, 0, True))
    got(xq[2], xd[2])
    spread(2)
    loop(2, lambda u: stat_tile(u, 1, True, 1))
    loop(2, lambda u: stat_tile(2 + u, 1, True))
    got(p_cps[3], p_cps[5], *pfar)
    relay_p(3, 5, 4)
    got(rp_cps[0], rp_cps[1], rp_cps[7], rp_cps[2])
    got(rp_cps[6], rp_cps[3], rp_cps[5], rp_cps[4])
    loop(2, lambda u: stat_tile(4 + u, 0, False))
    st_cps = []

    def share(p):
        packed[p, 0:4, :] = st[p, 0:4, :ROWS]
        packed[p, 4:8, :] = st[p, 0:4, ROWS:]
        for j in range(1, XN):
            p2 = token_slot((PAIRS[p][0] - j) % XN)[0]
            st_cps.append(start(packed.at[p], sbuf.at[XN - 1 - j, p2], dev(j, 0, 0)))

    def shared(k, p, row):
        first = token_slot((PAIRS[p][0] + XN - 1 - k) % XN)[1] // ROWS
        r0, r1 = 4 * first + row, 4 * (1 - first) + row
        return jnp.concatenate([sbuf[k, p, r0 : r0 + 1, :], sbuf[k, p, r1 : r1 + 1, :]], 1)

    share(0)
    loop(2, lambda u: stat_tile(4 + u, 1, False))
    share(1)
    got(*st_cps)
    for i in range(2):
        parts = [[st[i, r : r + 1, :] for r in range(3)]]
        parts += [[shared(j, i, r) for r in range(3)] for j in range(XN - 1)]
        m = parts[0][0]
        for p in parts[1:]:
            m = jnp.maximum(m, p[0])
        l = jnp.zeros_like(m)
        w = jnp.zeros_like(m)
        for p in parts:
            a = jnp.exp2(p[0] - m)
            l = l + p[1] * a
            w = w + p[2] * a
        norm[i, 0:1, :] = m + jnp.log2(l)
        norm[i, 1:2, :] = w / l

    def grad_tile(e, u, i, lo=0, n=UNIT):
        kk = keys[u, lo : lo + n]
        qrow, drow = qs[i], ds[i]
        p = jnp.exp2(logit[u, i, lo : lo + n] - norm[i, 0:1, :])
        dp = second[u - 4, i] if u >= 4 else nt(kk[:, DH:], drow)
        dl = (p * (dp - norm[i, 1:2, :])).astype(bf)
        acc[e, :n, :DH] += nn(dl, qrow)
        acc[e, :n, DH:] += nn(p.astype(bf), drow)
        dqt[i] += tn(kk[:, :DH], dl)

    pair_cps, z_cps = {}, {}

    def emit(e, n, tiles):
        for t in range(tiles):
            r = (t * 2 + 1) * n
            pair_s[e, t * n : (t + 1) * n, :DH] = (acc[e, r : r + n, :DH] * SCALE).astype(bf)
            pair_s[e, t * n : (t + 1) * n, DH:] = acc[e, r : r + n, DH:].astype(bf)
        rows = pl.ds(0, n * tiles)
        pair_cps[e] = start(pair_s.at[e, rows], pair_r.at[e, rows], peer)

    v_cps = {}
    summed = set()

    def forward(e, n, tiles, own, zin, via, via4):
        if e not in summed:
            got(pair_cps[e])
            summed.add(e)
        half = n // 2
        for t, o in tiles:
            rows = slice(t * n, (t + 1) * n)
            mine_k = acc[e, t * 2 * n : (t * 2 + 1) * n, :DH] * SCALE
            mine_v = acc[e, t * 2 * n : (t * 2 + 1) * n, DH:]
            both = jnp.concatenate([mine_k, mine_v], 1) + pair_r[e, rows, :].astype(f32)
            if o == 0:
                own[...] = both
                continue
            if o in (2, 6):
                w = 0 if o == 2 else 1
                got(v_cps[(n, 3 + 2 * w)], v_cps[(n, 4, w)])
                extra = via4[w].astype(f32)
                none = jnp.zeros_like(extra)
                extra = jnp.concatenate([none, extra] if w else [extra, none], 0)
                both = both + via[w].astype(f32) + extra
            zs[e, rows, :] = both.astype(bf)
            src = zs.at[e, pl.ds(t * n, n)]
            if o == 3:
                v_cps[(n, 3)] = start(src, via.at[0], dev(0, 1, 0))
            elif o == 5:
                v_cps[(n, 5)] = start(src, via.at[1], dev(0, 7, 0))
            elif o == 4:
                v_cps[(n, 4, 0)] = start(zs.at[e, pl.ds(t * n, half)], via4.at[0], dev(0, 2, 0))
                v_cps[(n, 4, 1)] = start(zs.at[e, pl.ds(t * n + half, half)], via4.at[1], dev(0, 6, 0))
            else:
                z_cps[(e, o)] = start(src, zin.at[ZN - 1 - o], dev(0, o, 0))

    def forward_p(e, *tiles):
        forward(e, PTOK, tiles, own_p, zin_p, via_p, via_p4)

    def forward_c(e, *tiles):
        forward(e, TOK, tiles, own_c, zin_c, via_c, via_c4)

    dq_cps = []

    def put_query(i):
        p, at = token_slot(i)
        for h in range(H):
            part = dqt[p, :, at + h * TOK : at + (h + 1) * TOK].T * SCALE
            dqs[i, :, h * DH : (h + 1) * DH] = part.astype(bf)
        if i:
            dq_cps.append(start(dqs.at[i], dqr.at[XN - 1 - i], dev(i, 0, 0)))

    loop(2, lambda i: grad_tile(5, 5, i))
    emit(5, PTOK, 4)
    loop(2, lambda i: grad_tile(4, 4, i))
    emit(4, PTOK, 4)
    forward_p(5, (1, 3), (2, 5), (3, 4))
    loop(2, lambda i: grad_tile(3, 3, i, 0, UNIT // 2))
    emit(3, TOK, 1)
    forward_p(4, (0, 0), (1, 1), (2, 7))
    loop(2, lambda i: grad_tile(2, 2, i))
    emit(2, TOK, 2)
    forward_c(3, (0, 4))
    forward_p(4, (3, 2))
    forward_p(5, (0, 6))
    loop(2, lambda i: grad_tile(1, 1, i))
    emit(1, TOK, 2)
    forward_c(2, (0, 3), (1, 5))
    grad_tile(0, 0, 1)
    grad_tile(6, 3, 1, UNIT // 2, UNIT // 2)
    put_query(2)
    put_query(0)
    forward_c(1, (0, 2), (1, 6))
    got(*[cp for (e, o), cp in z_cps.items() if e in (4, 5)])
    total = own_p[...]
    for j in (0, 1, 5, 6):
        total = total + zin_p[j].astype(f32)
    yslots[0] = total.astype(bf)
    my_cps = [start(yslots.at[0], yslots.at[GN - j], dev(0, 0, 0, j)) for j in range(1, GN)]
    grad_tile(0, 0, 0)
    emit(0, TOK, 2)
    grad_tile(6, 3, 0, UNIT // 2, UNIT // 2)
    emit(6, TOK, 1)
    put_query(1)
    put_query(3)
    forward_c(0, (0, 1), (1, 7))
    forward_c(6, (0, 0))
    got(*my_cps)
    total = jnp.zeros((PTOK, 2 * DH), f32)
    wanted = owned[g]
    for i in range(GN):
        w = (wanted == lax.rem(g + i, GN)).astype(f32)
        total = total + yslots[i].astype(f32) * w
    dp_out[...] = total.astype(bf)
    got(*dq_cps)
    total = dqs[0].astype(f32)
    for j in range(XN - 1):
        total = total + dqr[j].astype(f32)
    dq_out[...] = total.astype(bf)
    got(*[cp for (e, o), cp in z_cps.items() if e not in (4, 5)])
    total = own_c[...]
    for j in (0, 1, 5, 6):
        total = total + zin_c[j].astype(f32)
    dc_out[...] = total.astype(bf)
    for cp in everyone:
        cp.wait_send()


def hand_over(*refs):
    for i in range(3):
        refs[3 + i][0] = refs[i][...]


def shards(queries, comp_kv, out_grad, comp_ids, comp_pos, prompt_kv, owned_prompt):
    bf, f32, i32 = jnp.bfloat16, jnp.float32, jnp.int32
    hbm = pl.BlockSpec(memory_space=pl.ANY)
    vmem = pl.BlockSpec(memory_space=pltpu.VMEM)
    smem = pl.BlockSpec(memory_space=pltpu.SMEM)
    grad_q, grad_c, grad_p = pl.pallas_call(
        kernel,
        out_shape=[
            jax.ShapeDtypeStruct((TOK, ROWS), bf),
            jax.ShapeDtypeStruct((TOK, 2 * DH), bf),
            jax.ShapeDtypeStruct((PTOK, 2 * DH), bf),
        ],
        in_specs=[smem, vmem, vmem] + [hbm] * 4,
        out_specs=[vmem] * 3,
        scratch_shapes=[
            pltpu.VMEM((8, TOK), i32),
            pltpu.VMEM((XN, TOK, ROWS), bf),
            pltpu.VMEM((XN, TOK, ROWS), bf),
            pltpu.VMEM((XN, 8, TOK), i32),
            pltpu.VMEM((16, 8, TOK), i32),
            pltpu.VMEM((6, UNIT, 2 * DH), bf),
            pltpu.VMEM((4, UNIT, TOK), i32),
            pltpu.VMEM((2, WIDE, DH), bf),
            pltpu.VMEM((2, WIDE, DH), bf),
            pltpu.VMEM((GN, PTOK, 2 * DH), bf),
            pltpu.VMEM((PTOK, 2 * DH), bf),
            pltpu.VMEM((2, 8, WIDE), f32),
            pltpu.VMEM((2, 8, ROWS), f32),
            pltpu.VMEM((XN - 1, 2, 8, ROWS), f32),
            pltpu.VMEM((2, 8, WIDE), f32),
            pltpu.VMEM((6, 2, UNIT, WIDE), f32),
            pltpu.VMEM((2, 2, UNIT, WIDE), f32),
            pltpu.VMEM((7, UNIT, 2 * DH), f32),
            pltpu.VMEM((2, DH, WIDE), f32),
            pltpu.VMEM((TOK, 2 * DH), f32),
            pltpu.VMEM((PTOK, 2 * DH), f32),
            pltpu.VMEM((7, UNIT // 2, 2 * DH), bf),
            pltpu.VMEM((7, UNIT // 2, 2 * DH), bf),
            pltpu.VMEM((7, UNIT // 2, 2 * DH), bf),
            pltpu.VMEM((ZN - 1, TOK, 2 * DH), bf),
            pltpu.VMEM((ZN - 1, PTOK, 2 * DH), bf),
            pltpu.VMEM((2, TOK, 2 * DH), bf),
            pltpu.VMEM((2, TOK // 2, 2 * DH), bf),
            pltpu.VMEM((2, PTOK, 2 * DH), bf),
            pltpu.VMEM((2, PTOK // 2, 2 * DH), bf),
            pltpu.VMEM((XN, TOK, ROWS), bf),
            pltpu.VMEM((XN - 1, TOK, ROWS), bf),
            pltpu.VMEM((GN, PTOK, 2 * DH), bf),
            pltpu.SemaphoreType.DMA((N_SEM,)),
            pltpu.SemaphoreType.DMA((N_SEM,)),
            pltpu.SemaphoreType.DMA((4,)),
        ],
        compiler_params=pltpu.CompilerParams(
            collective_id=0, has_side_effects=True, vmem_limit_bytes=64 * 1024 * 1024
        ),
    )(owned_prompt, comp_ids, comp_pos, queries[0], out_grad[0], comp_kv[0], prompt_kv[0])
    results = (grad_q, grad_c, grad_p)
    return pl.pallas_call(
        hand_over,
        out_shape=[jax.ShapeDtypeStruct((1,) + r.shape, r.dtype) for r in results],
        in_specs=[vmem] * 3,
        out_specs=[vmem] * 3,
        compiler_params=pltpu.CompilerParams(vmem_limit_bytes=64 * 1024 * 1024),
    )(*results)


def solution(mesh):
    placed = (
        P("grp", "seq", None),
        P("grp", "seq", None),
        P("grp", "seq", None),
        P("grp", "seq"),
        P("grp", "seq"),
        P("grp", "seq", None),
        P(),
    )
    return jax.shard_map(
        shards,
        mesh=mesh,
        in_specs=placed,
        out_specs=(P("grp", "seq", None), P("grp", "seq", None), P("grp", "seq", None)),
        check_vma=False,
    )
```
